128 devices in a mesh: gx: 4 (over z_hi, core), gy: 4 (over x), gz: 8 (over y, z_lo).
Axes of the slice: x: 4, y: 4, z: 4 (z_hi: 2, z_lo: 2; z = z_hi * 2 + z_lo), core: 2. Of those that a mesh axis runs over, the one named last changes fastest.
Arguments:
- orbitals: float32 [2, 128, 512, 512], P(None, 'gz', 'gx', 'gy'), may hold values from -6 to 6
- potential: float32 [128, 512, 512], P('gz', 'gx', 'gy'), may hold values from -5 to 5
- counts: int32 [128, 27], P(('gx', 'gy', 'gz')), may hold values from 1 to 4, 48 in all within a row
- slot_atom: int32 [128, 27, 4], P(('gx', 'gy', 'gz')), may hold values from 0 to 15
- slot_block: int32 [128, 27, 4, 12], P(('gx', 'gy', 'gz')), may hold values from 0 to 2047
- projectors: float32 [128, 27, 4, 4, 1536], P(('gx', 'gy', 'gz')), may hold values from -0.6 to 0.6
- nl_energy: float32 [2048, 4], P(('gx', 'gy', 'gz')), may hold values from -1.5 to 1.5
Outputs:
- density: float32 [128, 512, 512], P('gz', 'gx', 'gy')
The draws below stay inside these ranges and needn't reach their ends.
Inputs may be any that keep to these rules, and one draw needn't show every extreme that they name: counts[d, j] slots of group j of brick d are used; each row sums to 48 and its largest entry is 4; groups whose owner lies outside the slab along z are ignored.
All inputs are finite; a program needn't handle non-finite values.
Results may differ from the reference program's by a relative error of at most 0.00025.
Values sent between devices are 32-bit elements; how exact they have to be, the bound alone decides.
A program may use at most 128 MiB of HBM per device.

```python
import math
import jax
import jax.numpy as jnp
import numpy as np
from jax import lax

ORB = 2
NPROJ = 4
NEIGH = 27
BZ = 16
BX = 128
BY = 128
ATOM_DEV = 16
CAP = 4
USED = 48
K = 12
NBLK = 2048
NZ = 128
NX = 512
NY = 512
NATOM = 2048
N_GX = 4
N_GY = 4
N_GZ = 8
DEVICES = 128


def touch_ends(entries, key, smallest, top_value):
    place = [jax.random.randint(jax.random.fold_in(key, axis), (), 0, length) for axis, length in enumerate(entries.shape)]
    longest = entries.shape.index(max(entries.shape))
    beside = place[:longest] + [(place[longest] + 1) % entries.shape[longest]] + place[longest + 1:]
    return entries.at[tuple(place)].set(smallest).at[tuple(beside)].set(top_value)


def level_of(own_key, shape, shards, least, largest):
    loudness = 1.0
    for position, blocks in shards:
        heights = jax.random.uniform(jax.random.fold_in(jax.random.fold_in(own_key, 6), position), (blocks,), jnp.float32, least / len(shards), largest / len(shards))
        loudness = loudness * jnp.repeat(jnp.exp(heights), shape[position] // blocks).reshape((-1,) + (1,) * (len(shape) - 1 - position))
    return loudness


def length_profile(amount, total, most, slope):
    weights = [(1 << 20) // math.isqrt(rank ** slope) + 1 for rank in range(2, amount + 1)]
    rest, given = total - most - (amount - 1), [1] * (amount - 1)
    while rest > 0:
        movable = [i for i in range(amount - 1) if given[i] < most]
        mass, remaining = sum([weights[i] for i in movable]), rest
        for i in movable:
            extra = min(most - given[i], max(1, remaining * weights[i] // mass), rest)
            given[i] = given[i] + extra
            rest = rest - extra
    return np.array([most] + given)


def uneven_parts(own_key, number_of, total, limit, lean):
    if number_of == 2:
        one = jax.random.randint(own_key, (), max(1, total - limit), min(limit, total - 1) + 1)
        return jnp.stack([one, total - one])
    tallies = jnp.asarray(length_profile(number_of, total, limit, lean), jnp.int32)
    pairs = (number_of - 1) // 2
    donor, taker = tallies[1:1 + 2 * pairs:2], tallies[2:2 + 2 * pairs:2]
    margin = jnp.minimum(donor - 1, limit - taker)
    shifted = jax.random.randint(jax.random.fold_in(own_key, 1), (pairs,), 0, 1 << 20) % (margin + 1)
    tallies = tallies.at[1:1 + 2 * pairs:2].set(donor - shifted).at[2:2 + 2 * pairs:2].set(taker + shifted)
    return tallies[jax.random.permutation(jax.random.fold_in(own_key, 2), number_of)]


def noise(stream_key, extent, spread, reach, cuts=(), kind=jnp.bfloat16):
    level = level_of(stream_key, extent, cuts, -0.22, 0.18) if cuts else 1.0
    drawn = jax.random.normal(stream_key, extent, jnp.float32) * spread * level
    return jnp.minimum(jnp.maximum(drawn, -reach), reach).astype(kind)


def setup_inputs(seed: int = 0) -> dict:
    arg_keys = jax.random.split(jax.random.key(seed), 8)
    orbitals = noise(arg_keys[0], (ORB, NZ, NX, NY), 1.0, 6.0, ((1, 8), (2, 4), (3, 4)), jnp.float32)
    potential = noise(arg_keys[1], (NZ, NX, NY), 1.0, 5.0, ((0, 8), (1, 4), (2, 4)), jnp.float32)
    counts = jax.vmap(lambda own: uneven_parts(own, NEIGH, USED, CAP, 2))(jax.random.split(arg_keys[2], DEVICES)).reshape((DEVICES, NEIGH)).astype(jnp.int32)
    slot_atom = touch_ends(jax.random.randint(arg_keys[3], (DEVICES, NEIGH, CAP), 0, ATOM_DEV), jax.random.fold_in(arg_keys[3], 1), 0, ATOM_DEV - 1).astype(jnp.int32)
    slot_block = touch_ends(jax.random.randint(arg_keys[4], (DEVICES, NEIGH, CAP, K), 0, NBLK), jax.random.fold_in(arg_keys[4], 1), 0, NBLK - 1).astype(jnp.int32)
    projectors = noise(arg_keys[5], (DEVICES, NEIGH, CAP, NPROJ, K * 128), 0.1, 0.6, ((0, 128),), jnp.float32)
    nl_energy = jnp.clip(jax.random.uniform(arg_keys[6], (NATOM, NPROJ), jnp.float32, -1.5, 1.5) * level_of(arg_keys[6], (NATOM, NPROJ), ((0, 128),), -0.4, 0.0), -1.5, 1.5)
    return dict(orbitals=orbitals, potential=potential, counts=counts, slot_atom=slot_atom, slot_block=slot_block, projectors=projectors, nl_energy=nl_energy)


CHEB_COEFS = (0.55, -0.62, 0.34, -0.18)
E_CENTER = 4.0
E_HALF = 7.0
highest = lax.Precision.HIGHEST


def laplace(padded):
    size_z = padded.shape[1] - 4
    size_x = padded.shape[2] - 4
    size_y = padded.shape[3] - 4

    def window(shift_z, shift_x, shift_y):
        return padded[:, 2 + shift_z:2 + shift_z + size_z, 2 + shift_x:2 + shift_x + size_x, 2 + shift_y:2 + shift_y + size_y]

    result = -90.0 * window(0, 0, 0)
    for offset, weight in ((1, 16.0), (-1, 16.0), (2, -1.0), (-2, -1.0)):
        result = result + weight * (window(offset, 0, 0) + window(0, offset, 0) + window(0, 0, offset))
    return result / 12.0


def to_bricks(wave_field):
    orb_count = wave_field.shape[0]
    bricks = wave_field.reshape(orb_count, N_GZ, BZ, N_GX, BX, N_GY, BY).transpose(3, 5, 1, 0, 2, 4, 6)
    return bricks.reshape(N_GX * N_GY * N_GZ, orb_count, -1, 128)


def from_bricks(bricks, orb_count):
    shaped = bricks.reshape(N_GX, N_GY, N_GZ, orb_count, BZ, BX, BY).transpose(3, 2, 4, 0, 5, 1, 6)
    return shaped.reshape(orb_count, N_GZ * BZ, N_GX * BX, N_GY * BY)


def pick_blocks(brick_rows, block_ids):
    return jnp.take(brick_rows, block_ids, axis=1)


def add_blocks(blank_rows, block_ids, contrib):
    return blank_rows.at[:, block_ids].add(contrib)


def reference(orbitals, potential, counts, slot_atom, slot_block, projectors, nl_energy):
    devices = N_GX * N_GY * N_GZ
    orb_count = orbitals.shape[0]
    groups = jnp.arange(27, dtype=jnp.int32)
    shift_x = groups // 9 - 1
    shift_y = (groups // 3) % 3 - 1
    shift_z = groups % 3 - 1
    device_ids = jnp.arange(devices, dtype=jnp.int32)
    index_x = device_ids // (N_GY * N_GZ)
    index_y = (device_ids // N_GZ) % N_GY
    index_z = device_ids % N_GZ
    target_z = index_z[:, None] + shift_z[None, :]
    inside = (target_z >= 0) & (target_z < N_GZ)
    owners = (((index_x[:, None] + shift_x[None, :]) % N_GX) * N_GY + (index_y[:, None] + shift_y[None, :]) % N_GY) * N_GZ + target_z
    live_slot = (jnp.arange(CAP, dtype=jnp.int32)[None, None, :] < counts[:, :, None]) & inside[:, :, None]
    atom_ids = jnp.where(live_slot, owners[:, :, None] * ATOM_DEV + slot_atom, 0).reshape(-1).astype(jnp.int32)
    live_f = live_slot.astype(jnp.float32)
    block_rows = slot_block.reshape(devices, -1).astype(jnp.int32)

    def apply_nonlocal(wave_field):
        bricks = to_bricks(wave_field)
        picked = jax.vmap(pick_blocks)(bricks, block_rows).reshape(devices, orb_count, 27, CAP, K * 128)
        coefficients = jnp.einsum('dgcpk,dogck->dgcpo', projectors, picked, precision=highest) * live_f[:, :, :, None, None]
        atom_sums = jax.ops.segment_sum(coefficients.reshape(-1, NPROJ, orb_count), atom_ids, num_segments=devices * ATOM_DEV)
        values = atom_sums * nl_energy[:, :, None]
        slot_values = values[atom_ids].reshape(devices, 27, CAP, NPROJ, orb_count) * live_f[:, :, :, None, None]
        contrib = jnp.einsum('dgcpk,dgcpo->dogck', projectors, slot_values, precision=highest).reshape(devices, orb_count, -1, 128)
        added_rows = jax.vmap(add_blocks)(jnp.zeros_like(bricks), block_rows, contrib)
        return from_bricks(added_rows, orb_count)

    def scaled_h(wave_field):
        padded = jnp.pad(wave_field, ((0, 0), (2, 2), (0, 0), (0, 0)))
        padded = jnp.pad(padded, ((0, 0), (0, 0), (2, 2), (2, 2)), mode="wrap")
        energy = -0.5 * laplace(padded) + potential[None] * wave_field + apply_nonlocal(wave_field)
        return (energy - E_CENTER * wave_field) / E_HALF

    previous = orbitals
    current = scaled_h(orbitals)
    filtered = CHEB_COEFS[0] * previous + CHEB_COEFS[1] * current
    for degree in range(2, 4):
        following = 2.0 * scaled_h(current) - previous
        filtered = filtered + CHEB_COEFS[degree] * following
        previous, current = current, following
    return jnp.mean(filtered * filtered, axis=0)
```

```python
import jax
import jax.numpy as jnp
from jax import lax
from jax.experimental import pallas as pl
from jax.experimental.pallas import tpu as pltpu
from jax.sharding import PartitionSpec as P

F32, BF16, I32 = jnp.float32, jnp.bfloat16, jnp.int32
MESH = pl.DeviceIdType.MESH
NX_DEV, NY_DEV, NZ_DEV = 4, 4, 8
BZ, BX = 16, 128
USED, SUP, NP = 48, 12, 4
ROWS = USED * SUP
PAD_ROWS = 640
OFFSETS = [(j // 9 - 1, (j // 3) % 3 - 1, j % 3 - 1) for j in range(27)]
XO = 8
PX = BX + 16
CH = 32
C1 = -16.0 / 168.0
C2 = 1.0 / 168.0
C0 = -0.25 / 7.0


def split(value):
    high = value.astype(BF16)
    return high, (value - high.astype(F32)).astype(BF16)


def mm(a, b):
    return jnp.dot(a, b, preferred_element_type=F32)


def body(
    orb_hbm, pot_hbm, cnt, satom, sblock, proj_hbm, nle, out_hbm,
    t0, t1, t2, halo, edge, pot, proj, pj, picks, cb, chi, clo, hot,
    qm, gt, gm, a48, g48, vals, p1, r1, v2, r2, ys, yr, xs, xr, outb, erow,
    rowi, bl,
    sem_in, sem_out, zs, zr, xss, xrs, yss, yrs, s1s, s1r, s2s, s2r,
):
    gx, gy, gz = lax.axis_index("gx"), lax.axis_index("gy"), lax.axis_index("gz")

    def at(off):
        return (
            lax.rem(gx + (off[0] + NX_DEV), NX_DEV),
            lax.rem(gy + (off[1] + NY_DEV), NY_DEV),
            lax.rem(gz + (off[2] + NZ_DEV), NZ_DEV),
        )

    loads = [
        pltpu.make_async_copy(orb_hbm, t0.at[:, pl.ds(2, BZ), pl.ds(XO, BX), :], sem_in.at[0]),
        pltpu.make_async_copy(proj_hbm.at[0], proj, sem_in.at[1]),
        pltpu.make_async_copy(pot_hbm, pot, sem_in.at[2]),
    ]
    for copy in loads:
        copy.start()
    barrier = pltpu.get_barrier_semaphore()
    for j in range(27):
        if j != 13:
            pl.semaphore_signal(barrier, inc=1, device_id=at(OFFSETS[j]), device_id_type=MESH)

    lane = lax.broadcasted_iota(I32, (8, 128), 1)
    lane_c = lax.broadcasted_iota(I32, (CH, 128), 1)
    sides = ((0, 0, 1), (0, 0, -1))

    def z_copies(k, t):
        up = pltpu.make_async_remote_copy(
            src_ref=t.at[:, pl.ds(BZ, 2), pl.ds(XO, BX), :], dst_ref=halo.at[k, 0],
            send_sem=zs.at[k, 0], recv_sem=zr.at[k, 0], device_id=at((0, 0, 1)), device_id_type=MESH)
        down = pltpu.make_async_remote_copy(
            src_ref=t.at[:, pl.ds(2, 2), pl.ds(XO, BX), :], dst_ref=halo.at[k, 1],
            send_sem=zs.at[k, 1], recv_sem=zr.at[k, 1], device_id=at((0, 0, -1)), device_id_type=MESH)
        return up, down

    def z_send(k, t):
        up, down = z_copies(k, t)

        @pl.when(gz < NZ_DEV - 1)
        def _():
            up.start()

        @pl.when(gz > 0)
        def _():
            down.start()

    def z_receive(k, t):
        up, down = z_copies(k, t)

        @pl.when(gz > 0)
        def _():
            up.wait_recv()
            for o in range(2):
                for i in range(2):
                    t[o, i, pl.ds(XO, BX), :] = halo[k, 0, o, i]

        @pl.when(gz < NZ_DEV - 1)
        def _():
            down.wait_recv()
            for o in range(2):
                for i in range(2):
                    t[o, BZ + 2 + i, pl.ds(XO, BX), :] = halo[k, 1, o, i]

    def z_sent(k, t):
        up, down = z_copies(k, t)

        @pl.when(gz < NZ_DEV - 1)
        def _():
            up.wait_send()

        @pl.when(gz > 0)
        def _():
            down.wait_send()

    def xy_copies(k):
        made = []
        for d, step in ((0, 1), (1, -1)):
            made.append(pltpu.make_async_remote_copy(
                src_ref=xs.at[k, d], dst_ref=xr.at[k, d], send_sem=xss.at[k, d], recv_sem=xrs.at[k, d],
                device_id=at((step, 0, 0)), device_id_type=MESH))
            made.append(pltpu.make_async_remote_copy(
                src_ref=ys.at[k], dst_ref=yr.at[k, d], send_sem=yss.at[k, d], recv_sem=yrs.at[k, d],
                device_id=at((0, step, 0)), device_id_type=MESH))
        return made

    def xy_pack(k, t):
        def pack_y(z, _):
            packed = jnp.zeros((8, 128), F32)
            for o in range(2):
                for i in range(16):
                    q = o * 16 + i
                    rolled = pltpu.roll(t[o, z + 2, pl.ds(XO + 8 * i, 8), :], (4 * q + 2) % 128, 1)
                    packed = jnp.where((lane >> 2) == q, rolled, packed)
            ys[k, z] = packed
            return 0

        def pack_x(pair, _):
            for half in range(2):
                for o in range(2):
                    q = half * 2 + o
                    xs[k, 0, pair, pl.ds(2 * q, 2), :] = t[o, 2 * pair + half + 2, pl.ds(XO + BX - 2, 2), :]
                    xs[k, 1, pair, pl.ds(2 * q, 2), :] = t[o, 2 * pair + half + 2, pl.ds(XO, 2), :]
            return 0

        lax.fori_loop(0, BZ // 2, pack_x, 0)
        lax.fori_loop(0, BZ, pack_y, 0)
        for copy in xy_copies(k):
            copy.start()

    def xy_unpack(k, t):
        for copy in xy_copies(k):
            copy.wait_recv()

        def unpack_y(z, _):
            merged = jnp.where((lane & 3) < 2, yr[k, 0, z], yr[k, 1, z])
            for o in range(2):
                for i in range(16):
                    q = o * 16 + i
                    edge[o, z, pl.ds(8 * i, 8), :] = pltpu.roll(merged, (126 - 4 * q) % 128, 1)
            return 0

        def unpack_x(pair, _):
            for half in range(2):
                for o in range(2):
                    q = half * 2 + o
                    t[o, 2 * pair + half + 2, pl.ds(XO - 2, 2), :] = xr[k, 0, pair, pl.ds(2 * q, 2), :]
                    t[o, 2 * pair + half + 2, pl.ds(XO + BX, 2), :] = xr[k, 1, pair, pl.ds(2 * q, 2), :]
            return 0

        lax.fori_loop(0, BZ // 2, unpack_x, 0)
        lax.fori_loop(0, BZ, unpack_y, 0)

    def first_round(k):
        made = []
        for j in range(27):
            if j != 13:
                made.append(pltpu.make_async_remote_copy(
                    src_ref=p1.at[k, j], dst_ref=r1.at[k, 26 - j], send_sem=s1s.at[k], recv_sem=s1r.at[k],
                    device_id=at(OFFSETS[j]), device_id_type=MESH))
        return made

    def second_round(k):
        made = []
        for j in range(27):
            if j != 13:
                made.append(pltpu.make_async_remote_copy(
                    src_ref=v2.at[k], dst_ref=r2.at[k, 26 - j], send_sem=s2s.at[k], recv_sem=s2r.at[k],
                    device_id=at(OFFSETS[j]), device_id_type=MESH))
        return made

    def all_rows(k, send, receive):
        return pltpu.make_async_remote_copy(
            src_ref=p1.at[k, pl.ds(0, 26)], dst_ref=r1.at[k, pl.ds(0, 26)], send_sem=send.at[k],
            recv_sem=receive.at[k], device_id=at((0, 0, 1)), device_id_type=MESH)

    def setup():
        def slot(k, state):
            j, s = state
            above = gz + lax.rem(j, 3) - 1
            live = (above >= 0) & (above < NZ_DEV)
            a48[pl.ds(k, 1), :] = jnp.full((1, 128), jnp.where(live, satom[0, j, s], -1000), I32)
            g48[pl.ds(k, 1), :] = jnp.full((1, 128), jnp.where(live, j, -1), I32)
            for i in range(SUP):
                block = sblock[0, j, s, i]
                rowi[i * USED + k] = (block >> 7) * PX + (block & 127) + (2 * PX + XO)
                bl[i * USED + k] = block
                pj[i, pl.ds(k, NP, stride=USED), :] = proj[j, s, :, pl.ds(i * 128, 128)]
            over = s + 1 >= cnt[0, j]
            return jnp.where(over, jnp.minimum(j + 1, 26), j), jnp.where(over, 0, s + 1)

        lax.fori_loop(0, USED, slot, (jnp.int32(0), jnp.int32(0)))
        lane48 = lax.broadcasted_iota(I32, (USED, 128), 1)
        group_hot = jnp.where(g48[...] == lane48, 1.0, 0.0)
        for po in range(8):
            qm[pl.ds(po * USED, USED), :] = jnp.where(a48[...] * 8 + po == lane48, 1.0, 0.0)
            gt[pl.ds(po * USED, USED), :] = group_hot.astype(BF16)
        for c in range(3):
            tall = gt[pl.ds(c * 128, 128), :].astype(F32)
            gm[:, pl.ds(c * 128, 128)] = tall.T[:32].astype(BF16)
        row = jnp.zeros((1, 128), F32)
        lane1 = lax.broadcasted_iota(I32, (1, 128), 1)
        for a in range(16):
            for p in range(NP):
                row = jnp.where((lane1 >> 1) == a * NP + p, nle[a, p], row)
        erow[...] = row
        vals[...] = jnp.zeros_like(vals)
        chi[pl.ds(ROWS, PAD_ROWS - ROWS), :] = jnp.zeros((PAD_ROWS - ROWS, 256), BF16)
        clo[pl.ds(ROWS, PAD_ROWS - ROWS), :] = jnp.zeros((PAD_ROWS - ROWS, 256), BF16)
        plane = jnp.zeros((BX, 128), F32)

        @pl.when(gz == 0)
        def _():
            for t in (t0, t1, t2):
                for o in range(2):
                    for i in range(2):
                        t[o, i, pl.ds(XO, BX), :] = plane

        @pl.when(gz == NZ_DEV - 1)
        def _():
            for t in (t0, t1, t2):
                for o in range(2):
                    for i in range(2):
                        t[o, BZ + 2 + i, pl.ds(XO, BX), :] = plane

    def setup_hot():
        lane1 = lax.broadcasted_iota(I32, (1, 128), 1)

        def fill(r, vectors):
            out = []
            for c in range(4):
                out.append(jnp.where(lane1 == r, bl[c * 128 + r], vectors[c]))
            out.append(jnp.where((lane1 == r) & (r < ROWS - 512), bl[jnp.minimum(512 + r, ROWS - 1)], vectors[4]))
            return tuple(out)

        vectors = lax.fori_loop(0, 128, fill, tuple(jnp.full((1, 128), -1, I32) for _ in range(5)), unroll=8)
        rows = lax.broadcasted_iota(I32, (BX, 128), 0)

        def plane(z, _):
            for c in range(5):
                hot[z, :, pl.ds(c * 128, 128)] = jnp.where(rows == vectors[c] - z * 128, 1.0, 0.0).astype(BF16)
            return 0

        lax.fori_loop(0, BZ, plane, 0)

    def coefficients(k, t):
        def gather(g, _):
            for s in range(8):
                row = rowi[g * 8 + s]
                z = row // PX
                for o in range(2):
                    picks[o, pl.ds(g * 8 + s, 1), :] = t[o, z, pl.ds(row - z * PX, 1), :]
            return 0

        lax.fori_loop(0, ROWS // 8, gather, 0)

        def reduce(g, _):
            for o in range(2):
                sums = [None] * NP
                for i in range(SUP):
                    pick = picks[o, pl.ds(i * USED + g * 8, 8), :]
                    for p in range(NP):
                        term = pj[i, pl.ds(p * USED + g * 8, 8), :] * pick
                        sums[p] = term if sums[p] is None else sums[p] + term
                for p in range(NP):
                    cb[pl.ds((p * 2 + o) * USED + g * 8, 8), :] = sums[p]
            return 0

        lax.fori_loop(0, USED // 8, reduce, 0)
        ones = jnp.ones((128, 128), BF16)
        high, low = split(cb[...])
        spread = (mm(high, ones) + mm(low, ones)) * qm[...]
        high, low = split(spread)
        part = mm(gm[...], high) + mm(gm[...], low)
        for j in range(27):
            if j == 13:
                r1[k, 13] = part[13:14]
            else:
                p1[k, j] = part[j:j + 1]
        for copy in first_round(k):
            copy.start()

    def totals(k):
        all_rows(k, s1s, s1r).wait_recv()
        row = r1[k, 0]
        for j in range(1, 27):
            row = row + r1[k, j]
        row = row * erow[...]
        v2[k] = row
        vals[pl.ds(13, 1), :] = row
        for copy in second_round(k):
            copy.start()

    def spread_values(k, factor):
        all_rows(k, s2s, s2r).wait_recv()
        for j in range(27):
            if j != 13:
                vals[pl.ds(j, 1), :] = r2[k, j]
        ones = jnp.ones((128, 128), BF16)
        high, low = split(vals[...] * factor)
        wide = (mm(gt[...], high) + mm(gt[...], low)) * qm[...]
        high, low = split(wide)
        cb[...] = mm(high, ones) + mm(low, ones)

        def expand(g, _):
            for o in range(2):
                weights = [cb[pl.ds((p * 2 + o) * USED + g * 16, 16), :] for p in range(NP)]
                for i in range(SUP):
                    total = weights[0] * pj[i, pl.ds(g * 16, 16), :]
                    for p in range(1, NP):
                        total = total + weights[p] * pj[i, pl.ds(p * USED + g * 16, 16), :]
                    high, low = split(total)
                    chi[pl.ds(i * USED + g * 16, 16), pl.ds(o * 128, 128)] = high
                    clo[pl.ds(i * USED + g * 16, 16), pl.ds(o * 128, 128)] = low
            return 0

        lax.fori_loop(0, USED // 16, expand, 0)

    def local_part(k, t, dest, before, z):
        def chunk(c, _):
            x0 = pl.multiple_of(c * CH, CH)
            here = pl.ds(XO + x0, CH)
            weight = pot[z, pl.ds(x0, CH), :] * (1.0 / 7.0) + C0
            for o in range(2):
                center = t[o, z + 2, here, :]
                e = edge[o, z, pl.ds(x0, CH), :]
                left = jnp.where(lane_c >= 126, e, center)
                right = jnp.where(lane_c < 2, e, center)
                near = (t[o, z + 1, here, :] + t[o, z + 3, here, :]) + (
                    t[o, z + 2, pl.ds(XO - 1 + x0, CH), :] + t[o, z + 2, pl.ds(XO + 1 + x0, CH), :])
                near = near + (pltpu.roll(jnp.where(lane_c == 127, e, center), 1, 1)
                               + pltpu.roll(jnp.where(lane_c == 0, e, center), 127, 1))
                far = (t[o, z, here, :] + t[o, z + 4, here, :]) + (
                    t[o, z + 2, pl.ds(XO - 2 + x0, CH), :] + t[o, z + 2, pl.ds(XO + 2 + x0, CH), :])
                far = far + (pltpu.roll(left, 2, 1) + pltpu.roll(right, 126, 1))
                value = C1 * near + C2 * far + weight * center
                if k == 0:
                    dest[o, z + 2, here, :] = value
                elif k == 1:
                    dest[o, z + 2, here, :] = 2.0 * value - before[o, z + 2, here, :]
                else:
                    dest[o, z + 2, here, :] = (
                        0.55 * t0[o, z + 2, here, :] - 0.44 * before[o, z + 2, here, :]
                        + 0.34 * center - 0.36 * value)
            return 0

        lax.fori_loop(0, BX // CH, chunk, 0)

    def add_nonlocal(k, dest, z):
        added = mm(hot[z], chi[...]) + mm(hot[z], clo[...])
        here = pl.ds(XO, BX)
        if k < 2:
            for o in range(2):
                dest[o, z + 2, here, :] = dest[o, z + 2, here, :] + added[:, o * 128:(o + 1) * 128]
        else:
            phi_a = dest[0, z + 2, here, :] + added[:, :128]
            phi_b = dest[1, z + 2, here, :] + added[:, 128:]
            outb[z] = 0.5 * (phi_a * phi_a + phi_b * phi_b)
            pltpu.make_async_copy(outb.at[z], out_hbm.at[z], sem_out.at[z]).start()

    loads[1].wait()
    setup()
    loads[0].wait()
    pl.semaphore_wait(barrier, 26)
    z_send(0, t0)
    xy_pack(0, t0)
    factors = (1.0 / 7.0, 2.0 / 7.0, -0.36 / 7.0)
    states = ((t0, t1, None), (t1, t2, t0), (t2, t0, t1))
    for k in range(3):
        t, dest, before = states[k]
        coefficients(k, t)
        xy_unpack(k, t)
        if k == 0:
            loads[2].wait()
            setup_hot()

        def inner(z, _):
            local_part(k, t, dest, before, z)
            return 0

        lax.fori_loop(2, BZ - 2, inner, 0)
        totals(k)
        spread_values(k, factors[k])
        z_receive(k, t)

        def outer(i, _):
            z = jnp.where(i < 2, i, i + (BZ - 4))
            local_part(k, t, dest, before, z)
            add_nonlocal(k, dest, z)
            return 0

        lax.fori_loop(0, 4, outer, 0)
        if k < 2:
            z_send(k + 1, dest)

        def finish(z, _):
            add_nonlocal(k, dest, z)
            return 0

        lax.fori_loop(2, BZ - 2, finish, 0)
        if k < 2:
            xy_pack(k + 1, dest)
        z_sent(k, t)
        for copy in xy_copies(k):
            copy.wait_send()
        all_rows(k, s1s, s1r).wait_send()
        all_rows(k, s2s, s2r).wait_send()
    for z in range(BZ):
        pltpu.make_async_copy(outb.at[z], out_hbm.at[z], sem_out.at[z]).wait()


def per_device(orbitals, potential, counts, slot_atom, slot_block, projectors, nl_energy):
    vmem, smem, anywhere = pltpu.VMEM, pltpu.SMEM, pl.BlockSpec(memory_space=pl.ANY)
    scalars = pl.BlockSpec(memory_space=pltpu.SMEM)
    field = vmem((2, BZ + 4, PX, 128), F32)
    dma = pltpu.SemaphoreType.DMA
    return pl.pallas_call(
        body,
        out_shape=jax.ShapeDtypeStruct(potential.shape, F32),
        in_specs=[anywhere, anywhere, scalars, scalars, scalars, anywhere, scalars],
        out_specs=anywhere,
        scratch_shapes=[
            field, field, field,
            vmem((3, 2, 2, 2, BX, 128), F32),
            vmem((2, BZ, BX, 128), F32),
            vmem((BZ, BX, 128), F32),
            vmem((27, 4, NP, SUP * 128), F32),
            vmem((SUP, NP * USED, 128), F32),
            vmem((2, ROWS, 128), F32),
            vmem((8 * USED, 128), F32),
            vmem((PAD_ROWS, 256), BF16), vmem((PAD_ROWS, 256), BF16),
            vmem((BZ, BX, PAD_ROWS), BF16),
            vmem((8 * USED, 128), F32), vmem((8 * USED, 128), BF16), vmem((32, 8 * USED), BF16),
            vmem((USED, 128), I32), vmem((USED, 128), I32),
            vmem((128, 128), F32),
            vmem((3, 27, 1, 128), F32), vmem((3, 27, 1, 128), F32),
            vmem((3, 1, 128), F32), vmem((3, 27, 1, 128), F32),
            vmem((3, BZ, 8, 128), F32), vmem((3, 2, BZ, 8, 128), F32),
            vmem((3, 2, BZ // 2, 8, 128), F32), vmem((3, 2, BZ // 2, 8, 128), F32),
            vmem((BZ, BX, 128), F32), vmem((1, 128), F32),
            smem((ROWS,), I32), smem((ROWS,), I32),
            dma((3,)), dma((BZ,)),
            dma((3, 2)), dma((3, 2)), dma((3, 2)), dma((3, 2)), dma((3, 2)), dma((3, 2)),
            dma((3,)), dma((3,)), dma((3,)), dma((3,)),
        ],
        compiler_params=pltpu.CompilerParams(
            collective_id=0, has_side_effects=True, vmem_limit_bytes=48 * 1024 * 1024
        ),
    )(orbitals, potential, counts, slot_atom, slot_block, projectors, nl_energy)


def solution(mesh):
    in_specs = (
        P(None, "gz", "gx", "gy"),
        P("gz", "gx", "gy"),
        P(("gx", "gy", "gz"), None),
        P(("gx", "gy", "gz"), None, None),
        P(("gx", "gy", "gz"), None, None, None),
        P(("gx", "gy", "gz"), None, None, None, None),
        P(("gx", "gy", "gz"), None),
    )
    out_specs = P("gz", "gx", "gy")
    return jax.shard_map(
        per_device, mesh=mesh, in_specs=in_specs, out_specs=out_specs, check_vma=False
    )
```

```python
import jax
import jax.numpy as jnp
from jax import lax
from jax.experimental import pallas as pl
from jax.experimental.pallas import tpu as pltpu
from jax.sharding import PartitionSpec as P

F32, BF16, I32 = jnp.float32, jnp.bfloat16, jnp.int32
MESH = pl.DeviceIdType.MESH
NX_DEV, NY_DEV, NZ_DEV = 4, 4, 8
BZ, BX = 16, 128
USED, SUP, NP = 48, 12, 4
ROWS = USED * SUP
PAD_ROWS = 640
OFFSETS = [(j // 9 - 1, (j // 3) % 3 - 1, j % 3 - 1) for j in range(27)]
FACES = (4, 22, 10, 16, 12, 14)
PLANES = (0, 1, 14, 15)
XO = 8
PX = BX + 16
CH = 64
C1 = -16.0 / 168.0
C2 = 1.0 / 168.0
C0 = -0.25 / 7.0


def split(value):
    high = value.astype(BF16)
    return high, (value - high.astype(F32)).astype(BF16)


def mm(a, b):
    return jnp.dot(a, b, preferred_element_type=F32)


def body(
    orb_hbm, pot_hbm, cnt_hbm, satom_hbm, sblock_hbm, proj_hbm, nle_hbm, out_hbm,
    t0, t1, t2, halo, edge, pot, proj, pj, picks, cb, chi, clo, hot,
    qm, gt, gm, a48, g48, vals, p1, r1, v2, r2, ys, yr, xs, xr, outb, erow,
    cnt, satom, sblock, nle, rowi,
    sem_y, sem_z, sem_in, sem_out, zs, zr, xss, xrs, yss, yrs, s1s, s1r, s2s, s2r,
):
    gx, gy, gz = lax.axis_index("gx"), lax.axis_index("gy"), lax.axis_index("gz")

    def at(off):
        return (
            lax.rem(gx + (off[0] + NX_DEV), NX_DEV),
            lax.rem(gy + (off[1] + NY_DEV), NY_DEV),
            lax.rem(gz + (off[2] + NZ_DEV), NZ_DEV),
        )

    loads = [
        pltpu.make_async_copy(orb_hbm, t0.at[:, pl.ds(2, BZ), pl.ds(XO, BX), :], sem_in.at[0]),
        pltpu.make_async_copy(proj_hbm.at[0], proj, sem_in.at[1]),
        pltpu.make_async_copy(pot_hbm, pot, sem_in.at[2]),
        pltpu.make_async_copy(cnt_hbm, cnt, sem_in.at[3]),
        pltpu.make_async_copy(satom_hbm, satom, sem_in.at[4]),
        pltpu.make_async_copy(sblock_hbm, sblock, sem_in.at[5]),
        pltpu.make_async_copy(nle_hbm, nle, sem_in.at[6]),
    ]
    for copy in loads:
        copy.start()
    barrier = pltpu.get_barrier_semaphore()
    for j in FACES:
        pl.semaphore_signal(barrier, inc=1, device_id=at(OFFSETS[j]), device_id_type=MESH)

    def greet(sem, pair):
        for j in pair:
            pl.semaphore_signal(sem, inc=1, device_id=at(OFFSETS[j]), device_id_type=MESH)
        pl.semaphore_wait(sem, 2)

    lane = lax.broadcasted_iota(I32, (8, 128), 1)
    lane_c = lax.broadcasted_iota(I32, (CH, 128), 1)
    sides = ((0, 0, 1), (0, 0, -1))

    def z_copies(k, t):
        up = pltpu.make_async_remote_copy(
            src_ref=t.at[:, pl.ds(BZ, 2), pl.ds(XO, BX), :], dst_ref=halo.at[k, 0],
            send_sem=zs.at[k, 0], recv_sem=zr.at[k, 0], device_id=at((0, 0, 1)), device_id_type=MESH)
        down = pltpu.make_async_remote_copy(
            src_ref=t.at[:, pl.ds(2, 2), pl.ds(XO, BX), :], dst_ref=halo.at[k, 1],
            send_sem=zs.at[k, 1], recv_sem=zr.at[k, 1], device_id=at((0, 0, -1)), device_id_type=MESH)
        return up, down

    def z_send(k, t):
        up, down = z_copies(k, t)

        @pl.when(gz < NZ_DEV - 1)
        def _():
            up.start()

        @pl.when(gz > 0)
        def _():
            down.start()

    def z_receive(k, t):
        up, down = z_copies(k, t)

        @pl.when(gz > 0)
        def _():
            up.wait_recv()
            for o in range(2):
                for i in range(2):
                    t[o, i, pl.ds(XO, BX), :] = halo[k, 0, o, i]

        @pl.when(gz < NZ_DEV - 1)
        def _():
            down.wait_recv()
            for o in range(2):
                for i in range(2):
                    t[o, BZ + 2 + i, pl.ds(XO, BX), :] = halo[k, 1, o, i]

    def z_sent(k, t):
        up, down = z_copies(k, t)

        @pl.when(gz < NZ_DEV - 1)
        def _():
            up.wait_send()

        @pl.when(gz > 0)
        def _():
            down.wait_send()

    def xy_copies(k):
        made = []
        for d, step in ((0, 1), (1, -1)):
            made.append(pltpu.make_async_remote_copy(
                src_ref=xs.at[k, d], dst_ref=xr.at[k, d], send_sem=xss.at[k, d], recv_sem=xrs.at[k, d],
                device_id=at((step, 0, 0)), device_id_type=MESH))
            made.append(pltpu.make_async_remote_copy(
                src_ref=ys.at[k], dst_ref=yr.at[k, d], send_sem=yss.at[k, d], recv_sem=yrs.at[k, d],
                device_id=at((0, step, 0)), device_id_type=MESH))
        return made

    def xy_pack(k, t):
        def pack_y(pair, _):
            for half in range(2):
                z = 2 * pair + half
                parts = []
                for first in range(0, 32, 8):
                    packed = None
                    for q in range(first, first + 8):
                        rolled = pltpu.roll(
                            t[q // 16, z + 2, pl.ds(XO + 8 * (q % 16), 8), :], (4 * q + 2) % 128, 1)
                        packed = rolled if packed is None else jnp.where((lane >> 2) == q, rolled, packed)
                    parts.append(packed)
                low = jnp.where((lane >> 5) == 0, parts[0], parts[1])
                high = jnp.where((lane >> 5) == 2, parts[2], parts[3])
                ys[k, z] = jnp.where((lane >> 6) == 0, low, high)
            return 0

        def pack_x(pair, _):
            for half in range(2):
                for o in range(2):
                    q = half * 2 + o
                    xs[k, 0, pair, pl.ds(2 * q, 2), :] = t[o, 2 * pair + half + 2, pl.ds(XO + BX - 2, 2), :]
                    xs[k, 1, pair, pl.ds(2 * q, 2), :] = t[o, 2 * pair + half + 2, pl.ds(XO, 2), :]
            return 0

        lax.fori_loop(0, BZ // 2, pack_x, 0)
        lax.fori_loop(0, BZ // 2, pack_y, 0)
        for copy in xy_copies(k):
            copy.start()

    def xy_unpack(k, t):
        for copy in xy_copies(k):
            copy.wait_recv()

        def unpack_y(pair, _):
            for half in range(2):
                z = 2 * pair + half
                merged = jnp.where((lane & 3) < 2, yr[k, 0, z], yr[k, 1, z])
                for q in range(32):
                    edge[q // 16, z, pl.ds(8 * (q % 16), 8), :] = pltpu.roll(merged, (126 - 4 * q) % 128, 1)
            return 0

        def unpack_x(pair, _):
            for half in range(2):
                for o in range(2):
                    q = half * 2 + o
                    t[o, 2 * pair + half + 2, pl.ds(XO - 2, 2), :] = xr[k, 0, pair, pl.ds(2 * q, 2), :]
                    t[o, 2 * pair + half + 2, pl.ds(XO + BX, 2), :] = xr[k, 1, pair, pl.ds(2 * q, 2), :]
            return 0

        lax.fori_loop(0, BZ // 2, unpack_x, 0)
        lax.fori_loop(0, BZ // 2, unpack_y, 0)

    def first_round(k):
        made = []
        for j in range(27):
            if j != 13:
                made.append(pltpu.make_async_remote_copy(
                    src_ref=p1.at[k, j], dst_ref=r1.at[k, 26 - j], send_sem=s1s.at[k], recv_sem=s1r.at[k],
                    device_id=at(OFFSETS[j]), device_id_type=MESH))
        return made

    def second_round(k):
        made = []
        for j in range(27):
            if j != 13:
                made.append(pltpu.make_async_remote_copy(
                    src_ref=v2.at[k], dst_ref=r2.at[k, 26 - j], send_sem=s2s.at[k], recv_sem=s2r.at[k],
                    device_id=at(OFFSETS[j]), device_id_type=MESH))
        return made

    def all_rows(k, send, receive):
        return pltpu.make_async_remote_copy(
            src_ref=p1.at[k, pl.ds(0, 26)], dst_ref=r1.at[k, pl.ds(0, 26)], send_sem=send.at[k],
            recv_sem=receive.at[k], device_id=at((0, 0, 1)), device_id_type=MESH)

    def setup():
        def slot(k, state):
            j, s, jz = state
            above = gz + jz - 1
            live = (above >= 0) & (above < NZ_DEV)
            a48[pl.ds(k, 1), :] = jnp.full((1, 128), jnp.where(live, satom[0, s, j], -1000), I32)
            g48[pl.ds(k, 1), :] = jnp.full((1, 128), jnp.where(live, j, -1), I32)
            for i in range(SUP):
                block = sblock[0, i, s, j]
                rowi[i * USED + k] = block + (block >> 7) * (PX - BX) + (2 * PX + XO)
                pj[i, pl.ds(k, NP, stride=USED), :] = proj[j, s, :, pl.ds(i * 128, 128)]
            over = s + 1 >= cnt[0, j]
            later = jnp.where(jz == 2, 0, jz + 1)
            return (jnp.where(over, jnp.minimum(j + 1, 26), j), jnp.where(over, 0, s + 1),
                    jnp.where(over, later, jz))

        lax.fori_loop(0, USED, slot, (jnp.int32(0), jnp.int32(0), jnp.int32(0)))
        lane48 = lax.broadcasted_iota(I32, (USED, 128), 1)
        group_hot = jnp.where(g48[...] == lane48, 1.0, 0.0)
        for po in range(8):
            qm[pl.ds(po * USED, USED), :] = jnp.where(a48[...] * 8 + po == lane48, 1.0, 0.0)
            gt[pl.ds(po * USED, USED), :] = group_hot.astype(BF16)
        for c in range(3):
            tall = gt[pl.ds(c * 128, 128), :].astype(F32)
            gm[:, pl.ds(c * 128, 128)] = tall.T[:32].astype(BF16)
        row = jnp.zeros((1, 128), F32)
        lane1 = lax.broadcasted_iota(I32, (1, 128), 1)
        for a in range(16):
            for p in range(NP):
                row = jnp.where((lane1 >> 1) == a * NP + p, nle[p, a], row)
        erow[...] = row
        vals[...] = jnp.zeros_like(vals)
        chi[pl.ds(ROWS, PAD_ROWS - ROWS), :] = jnp.zeros((PAD_ROWS - ROWS, 256), BF16)
        clo[pl.ds(ROWS, PAD_ROWS - ROWS), :] = jnp.zeros((PAD_ROWS - ROWS, 256), BF16)
        plane = jnp.zeros((BX, 128), F32)

        @pl.when(gz == 0)
        def _():
            for t in (t0, t1, t2):
                for o in range(2):
                    for i in range(2):
                        t[o, i, pl.ds(XO, BX), :] = plane

        @pl.when(gz == NZ_DEV - 1)
        def _():
            for t in (t0, t1, t2):
                for o in range(2):
                    for i in range(2):
                        t[o, BZ + 2 + i, pl.ds(XO, BX), :] = plane

    def setup_hot():
        lane1 = lax.broadcasted_iota(I32, (1, 128), 1)

        def fill(r, vectors):
            out = []
            for c in range(4):
                out.append(jnp.where(lane1 == r, rowi[c * 128 + r], vectors[c]))
            out.append(jnp.where((lane1 == r) & (r < ROWS - 512), rowi[jnp.minimum(512 + r, ROWS - 1)], vectors[4]))
            return tuple(out)

        vectors = lax.fori_loop(0, 128, fill, tuple(jnp.full((1, 128), -1, I32) for _ in range(5)), unroll=8)
        rows = lax.broadcasted_iota(I32, (BX, 128), 0)

        def plane(i, _):
            z = jnp.where(i < 2, i, jnp.where(i < 4, i + (BZ - 4), i - 2))
            for c in range(5):
                hot[i, :, pl.ds(c * 128, 128)] = jnp.where(
                    rows == vectors[c] - (z * PX + (2 * PX + XO)), 1.0, 0.0).astype(BF16)
            return 0

        lax.fori_loop(0, BZ, plane, 0)

    def coefficients(k, t):
        def gather(g, _):
            for s in range(8):
                row = rowi[g * 8 + s]
                for o in range(2):
                    picks[o, pl.ds(g * 8 + s, 1), :] = flat[o, pl.ds(row, 1), :]
            return 0

        flat = t.reshape(2, (BZ + 4) * PX, 128)
        lax.fori_loop(0, ROWS // 8, gather, 0, unroll=2)

        def reduce(g, _):
            for o in range(2):
                sums = [None] * NP
                for i in range(SUP):
                    pick = picks[o, pl.ds(i * USED + g * 8, 8), :]
                    for p in range(NP):
                        term = pj[i, pl.ds(p * USED + g * 8, 8), :] * pick
                        sums[p] = term if sums[p] is None else sums[p] + term
                for p in range(NP):
                    cb[pl.ds((p * 2 + o) * USED + g * 8, 8), :] = sums[p]
            return 0

        lax.fori_loop(0, USED // 8, reduce, 0)
        ones = jnp.ones((128, 128), BF16)
        high, low = split(cb[...])
        spread = (mm(high, ones) + mm(low, ones)) * qm[...]
        high, low = split(spread)
        part = mm(gm[...], high) + mm(gm[...], low)
        for j in range(27):
            if j == 13:
                r1[k, 13] = part[13:14]
            else:
                p1[k, j] = part[j:j + 1]
        for copy in first_round(k):
            copy.start()

    def totals(k):
        all_rows(k, s1s, s1r).wait_recv()
        row = r1[k, 0]
        for j in range(1, 27):
            row = row + r1[k, j]
        row = row * erow[...]
        v2[k] = row
        vals[pl.ds(13, 1), :] = row
        for copy in second_round(k):
            copy.start()

    def spread_values(k, factor):
        all_rows(k, s2s, s2r).wait_recv()
        for j in range(27):
            if j != 13:
                vals[pl.ds(j, 1), :] = r2[k, j]
        ones = jnp.ones((128, 128), BF16)
        high, low = split(vals[...] * factor)
        wide = (mm(gt[...], high) + mm(gt[...], low)) * qm[...]
        high, low = split(wide)
        cb[...] = mm(high, ones) + mm(low, ones)

        def expand(g, _):
            for o in range(2):
                weights = [cb[pl.ds((p * 2 + o) * USED + g * 16, 16), :] for p in range(NP)]
                for i in range(SUP):
                    total = weights[0] * pj[i, pl.ds(g * 16, 16), :]
                    for p in range(1, NP):
                        total = total + weights[p] * pj[i, pl.ds(p * USED + g * 16, 16), :]
                    high, low = split(total)
                    chi[pl.ds(i * USED + g * 16, 16), pl.ds(o * 128, 128)] = high
                    clo[pl.ds(i * USED + g * 16, 16), pl.ds(o * 128, 128)] = low
            return 0

        lax.fori_loop(0, USED // 16, expand, 0)

    def local_part(k, t, dest, before, z):
        def chunk(c, _):
            x0 = pl.multiple_of(c * CH, CH)
            here = pl.ds(XO + x0, CH)
            weight = pot[z, pl.ds(x0, CH), :] * (1.0 / 7.0) + C0
            for o in range(2):
                center = t[o, z + 2, here, :]
                e = edge[o, z, pl.ds(x0, CH), :]
                left = jnp.where(lane_c >= 126, e, center)
                right = jnp.where(lane_c < 2, e, center)
                near = (t[o, z + 1, here, :] + t[o, z + 3, here, :]) + (
                    t[o, z + 2, pl.ds(XO - 1 + x0, CH), :] + t[o, z + 2, pl.ds(XO + 1 + x0, CH), :])
                near = near + (pltpu.roll(jnp.where(lane_c == 127, e, center), 1, 1)
                               + pltpu.roll(jnp.where(lane_c == 0, e, center), 127, 1))
                far = (t[o, z, here, :] + t[o, z + 4, here, :]) + (
                    t[o, z + 2, pl.ds(XO - 2 + x0, CH), :] + t[o, z + 2, pl.ds(XO + 2 + x0, CH), :])
                far = far + (pltpu.roll(left, 2, 1) + pltpu.roll(right, 126, 1))
                value = C1 * near + C2 * far + weight * center
                if k == 0:
                    dest[o, z + 2, here, :] = value
                elif k == 1:
                    dest[o, z + 2, here, :] = 2.0 * value - before[o, z + 2, here, :]
                else:
                    dest[o, z + 2, here, :] = (
                        0.55 * t0[o, z + 2, here, :] - 0.44 * before[o, z + 2, here, :]
                        + 0.34 * center - 0.36 * value)
            return 0

        lax.fori_loop(0, BX // CH, chunk, 0)

    def add_nonlocal(k, dest, i, zs_of):
        four = hot[pl.ds(4 * i, 4)].reshape(4 * BX, PAD_ROWS)
        added = mm(four, chi[...]) + mm(four, clo[...])
        here = pl.ds(XO, BX)
        for n, z in enumerate(zs_of):
            rows = slice(n * BX, (n + 1) * BX)
            if k < 2:
                for o in range(2):
                    dest[o, z + 2, here, :] = dest[o, z + 2, here, :] + added[rows, o * 128:(o + 1) * 128]
            else:
                phi_a = dest[0, z + 2, here, :] + added[rows, :128]
                phi_b = dest[1, z + 2, here, :] + added[rows, 128:]
                outb[z] = 0.5 * (phi_a * phi_a + phi_b * phi_b)
                pltpu.make_async_copy(outb.at[z], out_hbm.at[z], sem_out.at[z]).start()

    loads[0].wait()
    pl.semaphore_wait(barrier, len(FACES))
    z_send(0, t0)
    greet(sem_y, (10, 16))
    for copy in loads[3:]:
        copy.wait()
    loads[1].wait()
    setup()
    greet(sem_z, (12, 14))
    factors = (1.0 / 7.0, 2.0 / 7.0, -0.36 / 7.0)
    states = ((t0, t1, None), (t1, t2, t0), (t2, t0, t1))
    for k in range(3):
        t, dest, before = states[k]
        coefficients(k, t)
        xy_pack(k, t)
        if k == 0:
            loads[2].wait()
            setup_hot()
        totals(k)
        xy_unpack(k, t)

        def inner(z, _):
            local_part(k, t, dest, before, z)
            return 0

        lax.fori_loop(2, BZ - 2, inner, 0)
        spread_values(k, factors[k])
        z_receive(k, t)

        def outer(i, _):
            local_part(k, t, dest, before, jnp.where(i < 2, i, i + (BZ - 4)))
            return 0

        lax.fori_loop(0, 4, outer, 0)
        add_nonlocal(k, dest, 0, PLANES)
        if k < 2:
            z_send(k + 1, dest)

        def finish(i, _):
            add_nonlocal(k, dest, i, [4 * i - 2 + n for n in range(4)])
            return 0

        lax.fori_loop(1, 4, finish, 0)
        z_sent(k, t)
        for copy in xy_copies(k):
            copy.wait_send()
        all_rows(k, s1s, s1r).wait_send()
        all_rows(k, s2s, s2r).wait_send()
    for z in range(BZ):
        pltpu.make_async_copy(outb.at[z], out_hbm.at[z], sem_out.at[z]).wait()


def per_device(orbitals, potential, counts, slot_atom, slot_block, projectors, nl_energy):
    vmem, smem, outside = pltpu.VMEM, pltpu.SMEM, pl.BlockSpec(memory_space=pltpu.HBM)
    field = vmem((2, BZ + 4, PX, 128), F32)
    dma = pltpu.SemaphoreType.DMA
    return pl.pallas_call(
        body,
        out_shape=jax.ShapeDtypeStruct(potential.shape, F32),
        in_specs=[outside] * 7,
        out_specs=outside,
        scratch_shapes=[
            field, field, field,
            vmem((3, 2, 2, 2, BX, 128), F32),
            vmem((2, BZ, BX, 128), F32),
            vmem((BZ, BX, 128), F32),
            vmem((27, 4, NP, SUP * 128), F32),
            vmem((SUP, NP * USED, 128), F32),
            vmem((2, ROWS, 128), F32),
            vmem((8 * USED, 128), F32),
            vmem((PAD_ROWS, 256), BF16), vmem((PAD_ROWS, 256), BF16),
            vmem((BZ, BX, PAD_ROWS), BF16),
            vmem((8 * USED, 128), F32), vmem((8 * USED, 128), BF16), vmem((32, 8 * USED), BF16),
            vmem((USED, 128), I32), vmem((USED, 128), I32),
            vmem((128, 128), F32),
            vmem((3, 27, 1, 128), F32), vmem((3, 27, 1, 128), F32),
            vmem((3, 1, 128), F32), vmem((3, 27, 1, 128), F32),
            vmem((3, BZ, 8, 128), F32), vmem((3, 2, BZ, 8, 128), F32),
            vmem((3, 2, BZ // 2, 8, 128), F32), vmem((3, 2, BZ // 2, 8, 128), F32),
            vmem((BZ, BX, 128), F32), vmem((1, 128), F32),
            smem((1, 27), I32), smem((1, 4, 27), I32), smem((1, SUP, 4, 27), I32), smem((NP, 16), F32),
            smem((ROWS,), I32),
            pltpu.SemaphoreType.REGULAR, pltpu.SemaphoreType.REGULAR, dma((7,)), dma((BZ,)),
            dma((3, 2)), dma((3, 2)), dma((3, 2)), dma((3, 2)), dma((3, 2)), dma((3, 2)),
            dma((3,)), dma((3,)), dma((3,)), dma((3,)),
        ],
        compiler_params=pltpu.CompilerParams(
            collective_id=0, has_side_effects=True, vmem_limit_bytes=63 * 1024 * 1024
        ),
    )(orbitals, potential, counts, slot_atom.transpose(0, 2, 1), slot_block.transpose(0, 3, 2, 1), projectors,
      nl_energy.T)


def solution(mesh):
    in_specs = (
        P(None, "gz", "gx", "gy"),
        P("gz", "gx", "gy"),
        P(("gx", "gy", "gz"), None),
        P(("gx", "gy", "gz"), None, None),
        P(("gx", "gy", "gz"), None, None, None),
        P(("gx", "gy", "gz"), None, None, None, None),
        P(("gx", "gy", "gz"), None),
    )
    out_specs = P("gz", "gx", "gy")
    return jax.shard_map(
        per_device, mesh=mesh, in_specs=in_specs, out_specs=out_specs, check_vma=False
    )
```

```python
import jax
import jax.numpy as jnp
from jax import lax
from jax.experimental import pallas as pl
from jax.experimental.pallas import tpu as pltpu
from jax.sharding import PartitionSpec as P

F32, BF16, I32 = jnp.float32, jnp.bfloat16, jnp.int32
MESH = pl.DeviceIdType.MESH
NX_DEV, NY_DEV, NZ_DEV = 4, 4, 8
BZ, BX = 16, 128
USED, SUP, NP = 48, 12, 4
ROWS = USED * SUP
PAD_ROWS = 640
OFFSETS = [(j // 9 - 1, (j // 3) % 3 - 1, j % 3 - 1) for j in range(27)]
FACES = (4, 22, 10, 16, 12, 14)
PLANES = (0, 1, 14, 15)
PARTS = ((0, 48), (48, 40), (88, 40))
XO = 8
PX = BX + 16
CH = 64
C1 = -16.0 / 168.0
C2 = 1.0 / 168.0
C0 = -0.25 / 7.0


def split(value):
    high = value.astype(BF16)
    return high, (value - high.astype(F32)).astype(BF16)


def mm(a, b):
    return jnp.dot(a, b, preferred_element_type=F32)


def body(
    orb_hbm, pot_hbm, cnt_hbm, satom_hbm, sblock_hbm, proj_hbm, nle_hbm, outb,
    t0, t1, t2, halo, edge, pot, proj, pj, picks, cb, chi, clo, hot,
    qm, gt, gm, a48, g48, vals, p1, r1, v2, r2, ys, yr, xs, xr, erow,
    cnt, satom, sblock, nle, rowi,
    sem_y, sem_z, sem_in, zs, zr, xss, xrs, yss, yrs, s1s, s1r, s2s, s2r,
):
    gx, gy, gz = lax.axis_index("gx"), lax.axis_index("gy"), lax.axis_index("gz")

    def at(off):
        return (
            lax.rem(gx + (off[0] + NX_DEV), NX_DEV),
            lax.rem(gy + (off[1] + NY_DEV), NY_DEV),
            lax.rem(gz + (off[2] + NZ_DEV), NZ_DEV),
        )

    loads = [
        pltpu.make_async_copy(orb_hbm, t0.at[:, pl.ds(2, BZ), pl.ds(XO, BX), :], sem_in.at[0]),
        pltpu.make_async_copy(proj_hbm.at[0], proj, sem_in.at[1]),
        pltpu.make_async_copy(pot_hbm, pot, sem_in.at[2]),
        pltpu.make_async_copy(cnt_hbm, cnt, sem_in.at[3]),
        pltpu.make_async_copy(satom_hbm, satom, sem_in.at[4]),
        pltpu.make_async_copy(sblock_hbm, sblock, sem_in.at[5]),
        pltpu.make_async_copy(nle_hbm, nle, sem_in.at[6]),
    ]
    for copy in loads:
        copy.start()
    barrier = pltpu.get_barrier_semaphore()
    for j in FACES:
        pl.semaphore_signal(barrier, inc=1, device_id=at(OFFSETS[j]), device_id_type=MESH)

    def greet(sem, pair):
        for j in pair:
            pl.semaphore_signal(sem, inc=1, device_id=at(OFFSETS[j]), device_id_type=MESH)
        pl.semaphore_wait(sem, 2)

    lane = lax.broadcasted_iota(I32, (8, 128), 1)
    lane_c = lax.broadcasted_iota(I32, (CH, 128), 1)
    sides = ((0, 0, 1), (0, 0, -1))

    def z_copy(k, t, up, part):
        first, count = PARTS[part]
        side = 0 if up else 1
        return pltpu.make_async_remote_copy(
            src_ref=t.at[:, pl.ds(BZ if up else 2, 2), pl.ds(XO + first, count), :],
            dst_ref=halo.at[k, side, :, :, pl.ds(first, count), :],
            send_sem=zs.at[k, side, part], recv_sem=zr.at[k, side, part],
            device_id=at((0, 0, 1 if up else -1)), device_id_type=MESH)

    def z_send(k, t, part):
        @pl.when(gz < NZ_DEV - 1)
        def _():
            z_copy(k, t, True, part).start()

        @pl.when(gz > 0)
        def _():
            z_copy(k, t, False, part).start()

    def z_receive(k, t):
        @pl.when(gz > 0)
        def _():
            for part in range(len(PARTS)):
                z_copy(k, t, True, part).wait_recv()
            for o in range(2):
                for i in range(2):
                    t[o, i, pl.ds(XO, BX), :] = halo[k, 0, o, i]

        @pl.when(gz < NZ_DEV - 1)
        def _():
            for part in range(len(PARTS)):
                z_copy(k, t, False, part).wait_recv()
            for o in range(2):
                for i in range(2):
                    t[o, BZ + 2 + i, pl.ds(XO, BX), :] = halo[k, 1, o, i]

    def z_sent(k, t):
        @pl.when(gz < NZ_DEV - 1)
        def _():
            for part in range(len(PARTS)):
                z_copy(k, t, True, part).wait_send()

        @pl.when(gz > 0)
        def _():
            for part in range(len(PARTS)):
                z_copy(k, t, False, part).wait_send()

    def xy_copies(k):
        made = []
        for d, step in ((0, 1), (1, -1)):
            made.append(pltpu.make_async_remote_copy(
                src_ref=xs.at[k, d], dst_ref=xr.at[k, d], send_sem=xss.at[k, d], recv_sem=xrs.at[k, d],
                device_id=at((step, 0, 0)), device_id_type=MESH))
            made.append(pltpu.make_async_remote_copy(
                src_ref=ys.at[k], dst_ref=yr.at[k, d], send_sem=yss.at[k, d], recv_sem=yrs.at[k, d],
                device_id=at((0, step, 0)), device_id_type=MESH))
        return made

    def xy_pack(k, t):
        def pack_y(pair, _):
            for half in range(2):
                z = 2 * pair + half
                parts = []
                for first in range(0, 32, 8):
                    packed = None
                    for q in range(first, first + 8):
                        rolled = pltpu.roll(
                            t[q // 16, z + 2, pl.ds(XO + 8 * (q % 16), 8), :], (4 * q + 2) % 128, 1)
                        packed = rolled if packed is None else jnp.where((lane >> 2) == q, rolled, packed)
                    parts.append(packed)
                low = jnp.where((lane >> 5) == 0, parts[0], parts[1])
                high = jnp.where((lane >> 5) == 2, parts[2], parts[3])
                ys[k, z] = jnp.where((lane >> 6) == 0, low, high)
            return 0

        def pack_x(pair, _):
            for half in range(2):
                for o in range(2):
                    q = half * 2 + o
                    xs[k, 0, pair, pl.ds(2 * q, 2), :] = t[o, 2 * pair + half + 2, pl.ds(XO + BX - 2, 2), :]
                    xs[k, 1, pair, pl.ds(2 * q, 2), :] = t[o, 2 * pair + half + 2, pl.ds(XO, 2), :]
            return 0

        lax.fori_loop(0, BZ // 2, pack_x, 0)
        lax.fori_loop(0, BZ // 2, pack_y, 0)
        for copy in xy_copies(k):
            copy.start()

    def xy_unpack(k, t):
        for copy in xy_copies(k):
            copy.wait_recv()

        def unpack_y(pair, _):
            for half in range(2):
                z = 2 * pair + half
                merged = jnp.where((lane & 3) < 2, yr[k, 0, z], yr[k, 1, z])
                for q in range(32):
                    edge[q // 16, z, pl.ds(8 * (q % 16), 8), :] = pltpu.roll(merged, (126 - 4 * q) % 128, 1)
            return 0

        def unpack_x(pair, _):
            for half in range(2):
                for o in range(2):
                    q = half * 2 + o
                    t[o, 2 * pair + half + 2, pl.ds(XO - 2, 2), :] = xr[k, 0, pair, pl.ds(2 * q, 2), :]
                    t[o, 2 * pair + half + 2, pl.ds(XO + BX, 2), :] = xr[k, 1, pair, pl.ds(2 * q, 2), :]
            return 0

        lax.fori_loop(0, BZ // 2, unpack_x, 0)
        lax.fori_loop(0, BZ // 2, unpack_y, 0)

    def first_round(k):
        made = []
        for j in range(27):
            if j != 13:
                made.append(pltpu.make_async_remote_copy(
                    src_ref=p1.at[k, j], dst_ref=r1.at[k, 26 - j], send_sem=s1s.at[k], recv_sem=s1r.at[k],
                    device_id=at(OFFSETS[j]), device_id_type=MESH))
        return made

    def second_round(k):
        made = []
        for j in range(27):
            if j != 13:
                made.append(pltpu.make_async_remote_copy(
                    src_ref=v2.at[k], dst_ref=r2.at[k, 26 - j], send_sem=s2s.at[k], recv_sem=s2r.at[k],
                    device_id=at(OFFSETS[j]), device_id_type=MESH))
        return made

    def all_rows(k, send, receive):
        return pltpu.make_async_remote_copy(
            src_ref=p1.at[k, pl.ds(0, 26)], dst_ref=r1.at[k, pl.ds(0, 26)], send_sem=send.at[k],
            recv_sem=receive.at[k], device_id=at((0, 0, 1)), device_id_type=MESH)

    def setup():
        def slot(k, state):
            j, s, jz = state
            above = gz + jz - 1
            live = (above >= 0) & (above < NZ_DEV)
            a48[pl.ds(k, 1), :] = jnp.full((1, 128), jnp.where(live, satom[0, s, j], -1000), I32)
            g48[pl.ds(k, 1), :] = jnp.full((1, 128), jnp.where(live, j, -1), I32)
            for i in range(SUP):
                block = sblock[0, i, s, j]
                rowi[i * USED + k] = block + (block >> 7) * (PX - BX) + (2 * PX + XO)
                pj[i, pl.ds(k, NP, stride=USED), :] = proj[j, s, :, pl.ds(i * 128, 128)]
            over = s + 1 >= cnt[0, j]
            later = jnp.where(jz == 2, 0, jz + 1)
            return (jnp.where(over, jnp.minimum(j + 1, 26), j), jnp.where(over, 0, s + 1),
                    jnp.where(over, later, jz))

        lax.fori_loop(0, USED, slot, (jnp.int32(0), jnp.int32(0), jnp.int32(0)))
        lane48 = lax.broadcasted_iota(I32, (USED, 128), 1)
        group_hot = jnp.where(g48[...] == lane48, 1.0, 0.0)
        for po in range(8):
            qm[pl.ds(po * USED, USED), :] = jnp.where(a48[...] * 8 + po == lane48, 1.0, 0.0)
            gt[pl.ds(po * USED, USED), :] = group_hot.astype(BF16)
        for c in range(3):
            tall = gt[pl.ds(c * 128, 128), :].astype(F32)
            gm[:, pl.ds(c * 128, 128)] = tall.T[:32].astype(BF16)
        row = jnp.zeros((1, 128), F32)
        lane1 = lax.broadcasted_iota(I32, (1, 128), 1)
        for a in range(16):
            for p in range(NP):
                row = jnp.where((lane1 >> 1) == a * NP + p, nle[p, a], row)
        erow[...] = row
        vals[...] = jnp.zeros_like(vals)
        chi[pl.ds(ROWS, PAD_ROWS - ROWS), :] = jnp.zeros((PAD_ROWS - ROWS, 256), BF16)
        clo[pl.ds(ROWS, PAD_ROWS - ROWS), :] = jnp.zeros((PAD_ROWS - ROWS, 256), BF16)
        plane = jnp.zeros((BX, 128), F32)

        @pl.when(gz == 0)
        def _():
            for t in (t0, t1, t2):
                for o in range(2):
                    for i in range(2):
                        t[o, i, pl.ds(XO, BX), :] = plane

        @pl.when(gz == NZ_DEV - 1)
        def _():
            for t in (t0, t1, t2):
                for o in range(2):
                    for i in range(2):
                        t[o, BZ + 2 + i, pl.ds(XO, BX), :] = plane

    def setup_hot():
        lane1 = lax.broadcasted_iota(I32, (1, 128), 1)

        def fill(r, vectors):
            out = []
            for c in range(4):
                out.append(jnp.where(lane1 == r, rowi[c * 128 + r], vectors[c]))
            out.append(jnp.where((lane1 == r) & (r < ROWS - 512), rowi[jnp.minimum(512 + r, ROWS - 1)], vectors[4]))
            return tuple(out)

        vectors = lax.fori_loop(0, 128, fill, tuple(jnp.full((1, 128), -1, I32) for _ in range(5)), unroll=8)
        rows = lax.broadcasted_iota(I32, (BX, 128), 0)

        def plane(i, _):
            z = jnp.where(i < 2, i, jnp.where(i < 4, i + (BZ - 4), i - 2))
            for c in range(5):
                hot[i, :, pl.ds(c * 128, 128)] = jnp.where(
                    rows == vectors[c] - (z * PX + (2 * PX + XO)), 1.0, 0.0).astype(BF16)
            return 0

        lax.fori_loop(0, BZ, plane, 0)

    def coefficients(k, t):
        def gather(g, _):
            for s in range(8):
                row = rowi[g * 8 + s]
                for o in range(2):
                    picks[o, pl.ds(g * 8 + s, 1), :] = flat[o, pl.ds(row, 1), :]
            return 0

        flat = t.reshape(2, (BZ + 4) * PX, 128)
        lax.fori_loop(0, ROWS // 8, gather, 0, unroll=2)

        def reduce(g, _):
            for o in range(2):
                sums = [None] * NP
                for i in range(SUP):
                    pick = picks[o, pl.ds(i * USED + g * 8, 8), :]
                    for p in range(NP):
                        term = pj[i, pl.ds(p * USED + g * 8, 8), :] * pick
                        sums[p] = term if sums[p] is None else sums[p] + term
                for p in range(NP):
                    cb[pl.ds((p * 2 + o) * USED + g * 8, 8), :] = sums[p]
            return 0

        lax.fori_loop(0, USED // 8, reduce, 0)
        ones = jnp.ones((128, 128), BF16)
        high, low = split(cb[...])
        spread = (mm(high, ones) + mm(low, ones)) * qm[...]
        high, low = split(spread)
        part = mm(gm[...], high) + mm(gm[...], low)
        for j in range(27):
            if j == 13:
                r1[k, 13] = part[13:14]
            else:
                p1[k, j] = part[j:j + 1]
        for copy in first_round(k):
            copy.start()

    def totals(k):
        all_rows(k, s1s, s1r).wait_recv()
        row = r1[k, 0]
        for j in range(1, 27):
            row = row + r1[k, j]
        row = row * erow[...]
        v2[k] = row
        vals[pl.ds(13, 1), :] = row
        for copy in second_round(k):
            copy.start()

    def spread_values(k, factor):
        all_rows(k, s2s, s2r).wait_recv()
        for j in range(27):
            if j != 13:
                vals[pl.ds(j, 1), :] = r2[k, j]
        ones = jnp.ones((128, 128), BF16)
        high, low = split(vals[...] * factor)
        wide = (mm(gt[...], high) + mm(gt[...], low)) * qm[...]
        high, low = split(wide)
        cb[...] = mm(high, ones) + mm(low, ones)

        def expand(g, _):
            for o in range(2):
                weights = [cb[pl.ds((p * 2 + o) * USED + g * 16, 16), :] for p in range(NP)]
                for i in range(SUP):
                    total = weights[0] * pj[i, pl.ds(g * 16, 16), :]
                    for p in range(1, NP):
                        total = total + weights[p] * pj[i, pl.ds(p * USED + g * 16, 16), :]
                    high, low = split(total)
                    chi[pl.ds(i * USED + g * 16, 16), pl.ds(o * 128, 128)] = high
                    clo[pl.ds(i * USED + g * 16, 16), pl.ds(o * 128, 128)] = low
            return 0

        lax.fori_loop(0, USED // 16, expand, 0)

    def local_part(k, t, dest, before, z):
        def chunk(c, _):
            x0 = pl.multiple_of(c * CH, CH)
            here = pl.ds(XO + x0, CH)
            weight = pot[z, pl.ds(x0, CH), :] * (1.0 / 7.0) + C0
            for o in range(2):
                center = t[o, z + 2, here, :]
                e = edge[o, z, pl.ds(x0, CH), :]
                left = jnp.where(lane_c >= 126, e, center)
                right = jnp.where(lane_c < 2, e, center)
                near = (t[o, z + 1, here, :] + t[o, z + 3, here, :]) + (
                    t[o, z + 2, pl.ds(XO - 1 + x0, CH), :] + t[o, z + 2, pl.ds(XO + 1 + x0, CH), :])
                near = near + (pltpu.roll(jnp.where(lane_c == 127, e, center), 1, 1)
                               + pltpu.roll(jnp.where(lane_c == 0, e, center), 127, 1))
                far = (t[o, z, here, :] + t[o, z + 4, here, :]) + (
                    t[o, z + 2, pl.ds(XO - 2 + x0, CH), :] + t[o, z + 2, pl.ds(XO + 2 + x0, CH), :])
                far = far + (pltpu.roll(left, 2, 1) + pltpu.roll(right, 126, 1))
                value = C1 * near + C2 * far + weight * center
                if k == 0:
                    dest[o, z + 2, here, :] = value
                elif k == 1:
                    dest[o, z + 2, here, :] = 2.0 * value - before[o, z + 2, here, :]
                else:
                    dest[o, z + 2, here, :] = (
                        0.55 * t0[o, z + 2, here, :] - 0.44 * before[o, z + 2, here, :]
                        + 0.34 * center - 0.36 * value)
            return 0

        lax.fori_loop(0, BX // CH, chunk, 0)

    def add_nonlocal(k, dest, i, zs_of):
        four = hot[pl.ds(4 * i, 4)].reshape(4 * BX, PAD_ROWS)
        added = mm(four, chi[...]) + mm(four, clo[...])
        here = pl.ds(XO, BX)
        for n, z in enumerate(zs_of):
            rows = slice(n * BX, (n + 1) * BX)
            if k < 2:
                for o in range(2):
                    dest[o, z + 2, here, :] = dest[o, z + 2, here, :] + added[rows, o * 128:(o + 1) * 128]
            else:
                phi_a = dest[0, z + 2, here, :] + added[rows, :128]
                phi_b = dest[1, z + 2, here, :] + added[rows, 128:]
                outb[z] = 0.5 * (phi_a * phi_a + phi_b * phi_b)

    loads[0].wait()
    pl.semaphore_wait(barrier, len(FACES))
    z_send(0, t0, 0)
    greet(sem_y, (10, 16))
    for copy in loads[3:]:
        copy.wait()
    loads[1].wait()
    setup()
    greet(sem_z, (12, 14))
    factors = (1.0 / 7.0, 2.0 / 7.0, -0.36 / 7.0)
    states = ((t0, t1, None), (t1, t2, t0), (t2, t0, t1))
    for k in range(3):
        t, dest, before = states[k]
        coefficients(k, t)
        xy_pack(k, t)
        z_send(k, t, 1)
        if k == 0:
            loads[2].wait()
            setup_hot()
        totals(k)
        z_send(k, t, 2)
        xy_unpack(k, t)

        def inner(z, _):
            local_part(k, t, dest, before, z)
            return 0

        lax.fori_loop(2, BZ - 2, inner, 0)
        spread_values(k, factors[k])
        z_receive(k, t)

        def outer(i, _):
            local_part(k, t, dest, before, jnp.where(i < 2, i, i + (BZ - 4)))
            return 0

        lax.fori_loop(0, 4, outer, 0)
        add_nonlocal(k, dest, 0, PLANES)
        if k < 2:
            z_send(k + 1, dest, 0)

        def finish(i, _):
            add_nonlocal(k, dest, i, [4 * i - 2 + n for n in range(4)])
            return 0

        lax.fori_loop(1, 4, finish, 0)
        z_sent(k, t)
        for copy in xy_copies(k):
            copy.wait_send()
        all_rows(k, s1s, s1r).wait_send()
        all_rows(k, s2s, s2r).wait_send()


def per_device(orbitals, potential, counts, slot_atom, slot_block, projectors, nl_energy):
    vmem, smem, outside = pltpu.VMEM, pltpu.SMEM, pl.BlockSpec(memory_space=pltpu.HBM)
    field = vmem((2, BZ + 4, PX, 128), F32)
    dma = pltpu.SemaphoreType.DMA
    return pl.pallas_call(
        body,
        out_shape=jax.ShapeDtypeStruct(potential.shape, F32),
        in_specs=[outside] * 7,
        out_specs=pl.BlockSpec(memory_space=pltpu.VMEM),
        scratch_shapes=[
            field, field, field,
            vmem((3, 2, 2, 2, BX, 128), F32),
            vmem((2, BZ, BX, 128), F32),
            vmem((BZ, BX, 128), F32),
            vmem((27, 4, NP, SUP * 128), F32),
            vmem((SUP, NP * USED, 128), F32),
            vmem((2, ROWS, 128), F32),
            vmem((8 * USED, 128), F32),
            vmem((PAD_ROWS, 256), BF16), vmem((PAD_ROWS, 256), BF16),
            vmem((BZ, BX, PAD_ROWS), BF16),
            vmem((8 * USED, 128), F32), vmem((8 * USED, 128), BF16), vmem((32, 8 * USED), BF16),
            vmem((USED, 128), I32), vmem((USED, 128), I32),
            vmem((128, 128), F32),
            vmem((3, 27, 1, 128), F32), vmem((3, 27, 1, 128), F32),
            vmem((3, 1, 128), F32), vmem((3, 27, 1, 128), F32),
            vmem((3, BZ, 8, 128), F32), vmem((3, 2, BZ, 8, 128), F32),
            vmem((3, 2, BZ // 2, 8, 128), F32), vmem((3, 2, BZ // 2, 8, 128), F32),
            vmem((1, 128), F32),
            smem((1, 27), I32), smem((1, 4, 27), I32), smem((1, SUP, 4, 27), I32), smem((NP, 16), F32),
            smem((ROWS,), I32),
            pltpu.SemaphoreType.REGULAR, pltpu.SemaphoreType.REGULAR, dma((7,)),
            dma((3, 2, 3)), dma((3, 2, 3)), dma((3, 2)), dma((3, 2)), dma((3, 2)), dma((3, 2)),
            dma((3,)), dma((3,)), dma((3,)), dma((3,)),
        ],
        compiler_params=pltpu.CompilerParams(
            collective_id=0, has_side_effects=True, vmem_limit_bytes=63 * 1024 * 1024
        ),
    )(orbitals, potential, counts, slot_atom.transpose(0, 2, 1), slot_block.transpose(0, 3, 2, 1), projectors,
      nl_energy.T)


def solution(mesh):
    in_specs = (
        P(None, "gz", "gx", "gy"),
        P("gz", "gx", "gy"),
        P(("gx", "gy", "gz"), None),
        P(("gx", "gy", "gz"), None, None),
        P(("gx", "gy", "gz"), None, None, None),
        P(("gx", "gy", "gz"), None, None, None, None),
        P(("gx", "gy", "gz"), None),
    )
    out_specs = P("gz", "gx", "gy")
    return jax.shard_map(
        per_device, mesh=mesh, in_specs=in_specs, out_specs=out_specs, check_vma=False
    )
```

```python
import jax
import jax.numpy as jnp
from jax import lax
from jax.experimental import pallas as pl
from jax.experimental.pallas import tpu as pltpu
from jax.sharding import PartitionSpec as P

F32, BF16, I32 = jnp.float32, jnp.bfloat16, jnp.int32
MESH = pl.DeviceIdType.MESH
NX_DEV, NY_DEV, NZ_DEV = 4, 4, 8
BZ, BX = 16, 128
USED, SUP, NP = 48, 12, 4
ROWS = USED * SUP
PAD_ROWS = 640
OFFSETS = [(j // 9 - 1, (j // 3) % 3 - 1, j % 3 - 1) for j in range(27)]
FACES = (4, 22, 10, 16, 12, 14)
PLANES = (0, 1, 14, 15)
PARTS = ((0, 48), (48, 40), (88, 40))
XO = 8
PX = BX + 16
CH = 16
C1 = -16.0 / 168.0
C2 = 1.0 / 168.0
C0 = -0.25 / 7.0


def split(value):
    high = value.astype(BF16)
    return high, (value - high.astype(F32)).astype(BF16)


def mm(a, b):
    return jnp.dot(a, b, preferred_element_type=F32)


def body(
    orb_hbm, pot_hbm, cnt_hbm, satom_hbm, sblock_hbm, proj_hbm, nle_hbm, outb,
    t0, t1, t2, halo, edge, pot, proj, pj, picks, cb, chi, clo, hot,
    qm, gt, gm, a48, g48, vals, p1, r1, v2, r2, ys, yr, xs, xr, erow,
    cnt, satom, sblock, nle, rowi,
    sem_y, sem_z, sem_in, zs, zr, xss, xrs, yss, yrs, s1s, s1r, s2s, s2r,
):
    gx, gy, gz = lax.axis_index("gx"), lax.axis_index("gy"), lax.axis_index("gz")

    def at(off):
        return (
            lax.rem(gx + (off[0] + NX_DEV), NX_DEV),
            lax.rem(gy + (off[1] + NY_DEV), NY_DEV),
            lax.rem(gz + (off[2] + NZ_DEV), NZ_DEV),
        )

    loads = [
        pltpu.make_async_copy(orb_hbm, t0.at[:, pl.ds(2, BZ), pl.ds(XO, BX), :], sem_in.at[0]),
        pltpu.make_async_copy(proj_hbm.at[0], proj, sem_in.at[1]),
        pltpu.make_async_copy(pot_hbm, pot, sem_in.at[2]),
        pltpu.make_async_copy(cnt_hbm, cnt, sem_in.at[3]),
        pltpu.make_async_copy(satom_hbm, satom, sem_in.at[4]),
        pltpu.make_async_copy(sblock_hbm, sblock, sem_in.at[5]),
        pltpu.make_async_copy(nle_hbm, nle, sem_in.at[6]),
    ]
    for copy in loads:
        copy.start()
    barrier = pltpu.get_barrier_semaphore()
    for j in FACES:
        pl.semaphore_signal(barrier, inc=1, device_id=at(OFFSETS[j]), device_id_type=MESH)

    def greet(sem, pair):
        for j in pair:
            pl.semaphore_signal(sem, inc=1, device_id=at(OFFSETS[j]), device_id_type=MESH)

    lane = lax.broadcasted_iota(I32, (8, 128), 1)
    lane_c = lax.broadcasted_iota(I32, (CH, 128), 1)
    sides = ((0, 0, 1), (0, 0, -1))

    def z_copy(k, t, up, part):
        first, count = PARTS[part]
        side = 0 if up else 1
        return pltpu.make_async_remote_copy(
            src_ref=t.at[:, pl.ds(BZ if up else 2, 2), pl.ds(XO + first, count), :],
            dst_ref=halo.at[k, side, :, :, pl.ds(first, count), :],
            send_sem=zs.at[k, side, part], recv_sem=zr.at[k, side, part],
            device_id=at((0, 0, 1 if up else -1)), device_id_type=MESH)

    def z_send(k, t, part):
        @pl.when(gz < NZ_DEV - 1)
        def _():
            z_copy(k, t, True, part).start()

        @pl.when(gz > 0)
        def _():
            z_copy(k, t, False, part).start()

    def z_receive(k, t, dest, factor):
        def add(o, z, value):
            here = pl.ds(XO, BX)
            dest[o, z + 2, here, :] = dest[o, z + 2, here, :] + value

        @pl.when(gz > 0)
        def _():
            for part in range(len(PARTS)):
                z_copy(k, t, True, part).wait_recv()
            for o in range(2):
                second, first = halo[k, 0, o, 0], halo[k, 0, o, 1]
                add(o, 0, (C1 * factor) * first + (C2 * factor) * second)
                add(o, 1, (C2 * factor) * first)

        @pl.when(gz < NZ_DEV - 1)
        def _():
            for part in range(len(PARTS)):
                z_copy(k, t, False, part).wait_recv()
            for o in range(2):
                first, second = halo[k, 1, o, 0], halo[k, 1, o, 1]
                add(o, BZ - 1, (C1 * factor) * first + (C2 * factor) * second)
                add(o, BZ - 2, (C2 * factor) * first)

    def z_sent(k, t):
        @pl.when(gz < NZ_DEV - 1)
        def _():
            for part in range(len(PARTS)):
                z_copy(k, t, True, part).wait_send()

        @pl.when(gz > 0)
        def _():
            for part in range(len(PARTS)):
                z_copy(k, t, False, part).wait_send()

    def xy_copies(k):
        made = []
        for d, step in ((0, 1), (1, -1)):
            made.append(pltpu.make_async_remote_copy(
                src_ref=xs.at[k, d], dst_ref=xr.at[k, d], send_sem=xss.at[k, d], recv_sem=xrs.at[k, d],
                device_id=at((step, 0, 0)), device_id_type=MESH))
            made.append(pltpu.make_async_remote_copy(
                src_ref=ys.at[k], dst_ref=yr.at[k, d], send_sem=yss.at[k, d], recv_sem=yrs.at[k, d],
                device_id=at((0, step, 0)), device_id_type=MESH))
        return made

    def xy_pack(k, t):
        def pack_y(pair, _):
            for half in range(2):
                z = 2 * pair + half
                parts = []
                for first in range(0, 32, 8):
                    packed = None
                    for q in range(first, first + 8):
                        rolled = pltpu.roll(
                            t[q // 16, z + 2, pl.ds(XO + 8 * (q % 16), 8), :], (4 * q + 2) % 128, 1)
                        packed = rolled if packed is None else jnp.where((lane >> 2) == q, rolled, packed)
                    parts.append(packed)
                low = jnp.where((lane >> 5) == 0, parts[0], parts[1])
                high = jnp.where((lane >> 5) == 2, parts[2], parts[3])
                ys[k, z] = jnp.where((lane >> 6) == 0, low, high)
            return 0

        def pack_x(pair, _):
            for half in range(2):
                for o in range(2):
                    q = half * 2 + o
                    xs[k, 0, pair, pl.ds(2 * q, 2), :] = t[o, 2 * pair + half + 2, pl.ds(XO + BX - 2, 2), :]
                    xs[k, 1, pair, pl.ds(2 * q, 2), :] = t[o, 2 * pair + half + 2, pl.ds(XO, 2), :]
            return 0

        lax.fori_loop(0, BZ // 2, pack_x, 0)
        lax.fori_loop(0, BZ // 2, pack_y, 0, unroll=2)
        for copy in xy_copies(k):
            copy.start()

    def xy_unpack(k, t):
        for copy in xy_copies(k):
            copy.wait_recv()

        def unpack_y(pair, _):
            for half in range(2):
                z = 2 * pair + half
                merged = jnp.where((lane & 3) < 2, yr[k, 0, z], yr[k, 1, z])
                for q in range(32):
                    edge[q // 16, z, pl.ds(8 * (q % 16), 8), :] = pltpu.roll(merged, (126 - 4 * q) % 128, 1)
            return 0

        def unpack_x(pair, _):
            for half in range(2):
                for o in range(2):
                    q = half * 2 + o
                    t[o, 2 * pair + half + 2, pl.ds(XO - 2, 2), :] = xr[k, 0, pair, pl.ds(2 * q, 2), :]
                    t[o, 2 * pair + half + 2, pl.ds(XO + BX, 2), :] = xr[k, 1, pair, pl.ds(2 * q, 2), :]
            return 0

        lax.fori_loop(0, BZ // 2, unpack_x, 0)
        lax.fori_loop(0, BZ // 2, unpack_y, 0, unroll=2)

    def first_round(k):
        made = []
        for j in range(27):
            if j != 13:
                made.append(pltpu.make_async_remote_copy(
                    src_ref=p1.at[k, j], dst_ref=r1.at[k, 26 - j], send_sem=s1s.at[k], recv_sem=s1r.at[k],
                    device_id=at(OFFSETS[j]), device_id_type=MESH))
        return made

    def second_round(k):
        made = []
        for j in range(27):
            if j != 13:
                made.append(pltpu.make_async_remote_copy(
                    src_ref=v2.at[k], dst_ref=r2.at[k, 26 - j], send_sem=s2s.at[k], recv_sem=s2r.at[k],
                    device_id=at(OFFSETS[j]), device_id_type=MESH))
        return made

    def all_rows(k, send, receive):
        return pltpu.make_async_remote_copy(
            src_ref=p1.at[k, pl.ds(0, 26)], dst_ref=r1.at[k, pl.ds(0, 26)], send_sem=send.at[k],
            recv_sem=receive.at[k], device_id=at((0, 0, 1)), device_id_type=MESH)

    def setup():
        def slot(k, state):
            j, s, jz = state
            above = gz + jz - 1
            live = (above >= 0) & (above < NZ_DEV)
            a48[pl.ds(k, 1), :] = jnp.full((1, 128), jnp.where(live, satom[0, s, j], -1000), I32)
            g48[pl.ds(k, 1), :] = jnp.full((1, 128), jnp.where(live, j, -1), I32)
            for i in range(SUP):
                block = sblock[0, i, s, j]
                rowi[i * USED + k] = block + (block >> 7) * (PX - BX) + (2 * PX + XO)
                pj[i, pl.ds(k, NP, stride=USED), :] = proj[j, s, :, pl.ds(i * 128, 128)]
            over = s + 1 >= cnt[0, j]
            later = jnp.where(jz == 2, 0, jz + 1)
            return (jnp.where(over, jnp.minimum(j + 1, 26), j), jnp.where(over, 0, s + 1),
                    jnp.where(over, later, jz))

        lax.fori_loop(0, USED, slot, (jnp.int32(0), jnp.int32(0), jnp.int32(0)))
        lane48 = lax.broadcasted_iota(I32, (USED, 128), 1)
        group_hot = jnp.where(g48[...] == lane48, 1.0, 0.0)
        for po in range(8):
            qm[pl.ds(po * USED, USED), :] = jnp.where(a48[...] * 8 + po == lane48, 1.0, 0.0)
            gt[pl.ds(po * USED, USED), :] = group_hot.astype(BF16)
        for c in range(3):
            tall = gt[pl.ds(c * 128, 128), :].astype(F32)
            gm[:, pl.ds(c * 128, 128)] = tall.T[:32].astype(BF16)
        row = jnp.zeros((1, 128), F32)
        lane1 = lax.broadcasted_iota(I32, (1, 128), 1)
        for a in range(16):
            for p in range(NP):
                row = jnp.where((lane1 >> 1) == a * NP + p, nle[p, a], row)
        erow[...] = row
        vals[...] = jnp.zeros_like(vals)
        chi[pl.ds(ROWS, PAD_ROWS - ROWS), :] = jnp.zeros((PAD_ROWS - ROWS, 256), BF16)
        clo[pl.ds(ROWS, PAD_ROWS - ROWS), :] = jnp.zeros((PAD_ROWS - ROWS, 256), BF16)
        plane = jnp.zeros((BX, 128), F32)

        for t in (t0, t1, t2):
            for o in range(2):
                for i in (0, 1, BZ + 2, BZ + 3):
                    t[o, i, pl.ds(XO, BX), :] = plane

    def setup_hot():
        lane1 = lax.broadcasted_iota(I32, (1, 128), 1)

        def fill(r, vectors):
            out = []
            for c in range(4):
                out.append(jnp.where(lane1 == r, rowi[c * 128 + r], vectors[c]))
            out.append(jnp.where((lane1 == r) & (r < ROWS - 512), rowi[jnp.minimum(512 + r, ROWS - 1)], vectors[4]))
            return tuple(out)

        vectors = lax.fori_loop(0, 128, fill, tuple(jnp.full((1, 128), -1, I32) for _ in range(5)), unroll=8)
        rows = lax.broadcasted_iota(I32, (BX, 128), 0)

        def plane(i, _):
            z = jnp.where(i < 2, i, jnp.where(i < 4, i + (BZ - 4), i - 2))
            for c in range(5):
                hot[i, :, pl.ds(c * 128, 128)] = jnp.where(
                    rows == vectors[c] - (z * PX + (2 * PX + XO)), 1.0, 0.0).astype(BF16)
            return 0

        lax.fori_loop(0, BZ, plane, 0)

    def coefficients(k, t):
        def gather(g, _):
            for s in range(8):
                row = rowi[g * 8 + s]
                for o in range(2):
                    picks[o, pl.ds(g * 8 + s, 1), :] = flat[o, pl.ds(row, 1), :]
            return 0

        flat = t.reshape(2, (BZ + 4) * PX, 128)
        lax.fori_loop(0, ROWS // 8, gather, 0, unroll=2)
        if k == 0:
            pl.semaphore_wait(sem_y, 2)
            greet(sem_z, (12, 14))

        def reduce(g, _):
            for o in range(2):
                sums = [None] * NP
                for i in range(SUP):
                    pick = picks[o, pl.ds(i * USED + g * 8, 8), :]
                    for p in range(NP):
                        term = pj[i, pl.ds(p * USED + g * 8, 8), :] * pick
                        sums[p] = term if sums[p] is None else sums[p] + term
                for p in range(NP):
                    cb[pl.ds((p * 2 + o) * USED + g * 8, 8), :] = sums[p]
            return 0

        lax.fori_loop(0, USED // 8, reduce, 0)
        ones = jnp.ones((128, 128), BF16)
        high, low = split(cb[...])
        spread = (mm(high, ones) + mm(low, ones)) * qm[...]
        high, low = split(spread)
        part = mm(gm[...], high) + mm(gm[...], low)
        for j in range(27):
            if j == 13:
                r1[k, 13] = part[13:14]
            else:
                p1[k, j] = part[j:j + 1]
        if k == 0:
            pl.semaphore_wait(sem_z, 2)
        for copy in first_round(k):
            copy.start()

    def totals(k):
        all_rows(k, s1s, s1r).wait_recv()
        row = r1[k, 0]
        for j in range(1, 27):
            row = row + r1[k, j]
        row = row * erow[...]
        v2[k] = row
        vals[pl.ds(13, 1), :] = row
        for copy in second_round(k):
            copy.start()

    def spread_values(k, factor):
        all_rows(k, s2s, s2r).wait_recv()
        for j in range(27):
            if j != 13:
                vals[pl.ds(j, 1), :] = r2[k, j]
        ones = jnp.ones((128, 128), BF16)
        high, low = split(vals[...] * factor)
        wide = (mm(gt[...], high) + mm(gt[...], low)) * qm[...]
        high, low = split(wide)
        cb[...] = mm(high, ones) + mm(low, ones)

        def expand(g, _):
            for o in range(2):
                weights = [cb[pl.ds((p * 2 + o) * USED + g * 16, 16), :] for p in range(NP)]
                for i in range(SUP):
                    total = weights[0] * pj[i, pl.ds(g * 16, 16), :]
                    for p in range(1, NP):
                        total = total + weights[p] * pj[i, pl.ds(p * USED + g * 16, 16), :]
                    high, low = split(total)
                    chi[pl.ds(i * USED + g * 16, 16), pl.ds(o * 128, 128)] = high
                    clo[pl.ds(i * USED + g * 16, 16), pl.ds(o * 128, 128)] = low
            return 0

        lax.fori_loop(0, USED // 16, expand, 0)

    def local_part(k, t, dest, before, z):
        def chunk(c, _):
            x0 = pl.multiple_of(c * CH, CH)
            here = pl.ds(XO + x0, CH)
            weight = pot[z, pl.ds(x0, CH), :] * (1.0 / 7.0) + C0
            for o in range(2):
                center = t[o, z + 2, here, :]
                e = edge[o, z, pl.ds(x0, CH), :]
                left = jnp.where(lane_c >= 126, e, center)
                right = jnp.where(lane_c < 2, e, center)
                near = (t[o, z + 1, here, :] + t[o, z + 3, here, :]) + (
                    t[o, z + 2, pl.ds(XO - 1 + x0, CH), :] + t[o, z + 2, pl.ds(XO + 1 + x0, CH), :])
                near = near + (pltpu.roll(jnp.where(lane_c == 127, e, center), 1, 1)
                               + pltpu.roll(jnp.where(lane_c == 0, e, center), 127, 1))
                far = (t[o, z, here, :] + t[o, z + 4, here, :]) + (
                    t[o, z + 2, pl.ds(XO - 2 + x0, CH), :] + t[o, z + 2, pl.ds(XO + 2 + x0, CH), :])
                far = far + (pltpu.roll(left, 2, 1) + pltpu.roll(right, 126, 1))
                value = C1 * near + C2 * far + weight * center
                if k == 0:
                    dest[o, z + 2, here, :] = value
                elif k == 1:
                    dest[o, z + 2, here, :] = 2.0 * value - before[o, z + 2, here, :]
                else:
                    dest[o, z + 2, here, :] = (
                        0.55 * t0[o, z + 2, here, :] - 0.44 * before[o, z + 2, here, :]
                        + 0.34 * center - 0.36 * value)
            return 0

        lax.fori_loop(0, BX // CH, chunk, 0, unroll=True)

    def add_nonlocal(k, dest, i, zs_of):
        four = hot[pl.ds(4 * i, 4)].reshape(4 * BX, PAD_ROWS)
        added = mm(four, chi[...]) + mm(four, clo[...])
        here = pl.ds(XO, BX)
        for n, z in enumerate(zs_of):
            rows = slice(n * BX, (n + 1) * BX)
            if k < 2:
                for o in range(2):
                    dest[o, z + 2, here, :] = dest[o, z + 2, here, :] + added[rows, o * 128:(o + 1) * 128]
            else:
                phi_a = dest[0, z + 2, here, :] + added[rows, :128]
                phi_b = dest[1, z + 2, here, :] + added[rows, 128:]
                outb[z] = 0.5 * (phi_a * phi_a + phi_b * phi_b)

    for copy in loads[3:]:
        copy.wait()
    loads[1].wait()
    setup()
    loads[0].wait()
    pl.semaphore_wait(barrier, len(FACES))
    z_send(0, t0, 0)
    greet(sem_y, (10, 16))
    factors = (1.0 / 7.0, 2.0 / 7.0, -0.36 / 7.0)
    states = ((t0, t1, None), (t1, t2, t0), (t2, t0, t1))
    for k in range(3):
        t, dest, before = states[k]
        coefficients(k, t)
        xy_pack(k, t)
        z_send(k, t, 1)
        if k == 0:
            loads[2].wait()
            setup_hot()
        totals(k)
        z_send(k, t, 2)
        xy_unpack(k, t)

        def inner(z, _):
            local_part(k, t, dest, before, z)
            return 0

        lax.fori_loop(0, BZ, inner, 0)
        spread_values(k, factors[k])
        z_receive(k, t, dest, (1.0, 2.0, -0.36)[k])
        add_nonlocal(k, dest, 0, PLANES)
        if k < 2:
            z_send(k + 1, dest, 0)

        def finish(i, _):
            add_nonlocal(k, dest, i, [4 * i - 2 + n for n in range(4)])
            return 0

        lax.fori_loop(1, 4, finish, 0)
        z_sent(k, t)
        for copy in xy_copies(k):
            copy.wait_send()
        all_rows(k, s1s, s1r).wait_send()
        all_rows(k, s2s, s2r).wait_send()


def per_device(orbitals, potential, counts, slot_atom, slot_block, projectors, nl_energy):
    vmem, smem, outside = pltpu.VMEM, pltpu.SMEM, pl.BlockSpec(memory_space=pltpu.HBM)
    field = vmem((2, BZ + 4, PX, 128), F32)
    dma = pltpu.SemaphoreType.DMA
    return pl.pallas_call(
        body,
        out_shape=jax.ShapeDtypeStruct(potential.shape, F32),
        in_specs=[outside] * 7,
        out_specs=pl.BlockSpec(memory_space=pltpu.VMEM),
        scratch_shapes=[
            field, field, field,
            vmem((3, 2, 2, 2, BX, 128), F32),
            vmem((2, BZ, BX, 128), F32),
            vmem((BZ, BX, 128), F32),
            vmem((27, 4, NP, SUP * 128), F32),
            vmem((SUP, NP * USED, 128), F32),
            vmem((2, ROWS, 128), F32),
            vmem((8 * USED, 128), F32),
            vmem((PAD_ROWS, 256), BF16), vmem((PAD_ROWS, 256), BF16),
            vmem((BZ, BX, PAD_ROWS), BF16),
            vmem((8 * USED, 128), F32), vmem((8 * USED, 128), BF16), vmem((32, 8 * USED), BF16),
            vmem((USED, 128), I32), vmem((USED, 128), I32),
            vmem((128, 128), F32),
            vmem((3, 27, 1, 128), F32), vmem((3, 27, 1, 128), F32),
            vmem((3, 1, 128), F32), vmem((3, 27, 1, 128), F32),
            vmem((3, BZ, 8, 128), F32), vmem((3, 2, BZ, 8, 128), F32),
            vmem((3, 2, BZ // 2, 8, 128), F32), vmem((3, 2, BZ // 2, 8, 128), F32),
            vmem((1, 128), F32),
            smem((1, 27), I32), smem((1, 4, 27), I32), smem((1, SUP, 4, 27), I32), smem((NP, 16), F32),
            smem((ROWS,), I32),
            pltpu.SemaphoreType.REGULAR, pltpu.SemaphoreType.REGULAR, dma((7,)),
            dma((3, 2, 3)), dma((3, 2, 3)), dma((3, 2)), dma((3, 2)), dma((3, 2)), dma((3, 2)),
            dma((3,)), dma((3,)), dma((3,)), dma((3,)),
        ],
        compiler_params=pltpu.CompilerParams(
            collective_id=0, has_side_effects=True, vmem_limit_bytes=63 * 1024 * 1024
        ),
    )(orbitals, potential, counts, slot_atom.transpose(0, 2, 1), slot_block.transpose(0, 3, 2, 1), projectors,
      nl_energy.T)


def solution(mesh):
    in_specs = (
        P(None, "gz", "gx", "gy"),
        P("gz", "gx", "gy"),
        P(("gx", "gy", "gz"), None),
        P(("gx", "gy", "gz"), None, None),
        P(("gx", "gy", "gz"), None, None, None),
        P(("gx", "gy", "gz"), None, None, None, None),
        P(("gx", "gy", "gz"), None),
    )
    out_specs = P("gz", "gx", "gy")
    return jax.shard_map(
        per_device, mesh=mesh, in_specs=in_specs, out_specs=out_specs, check_vma=False
    )
```

```python
import jax
import jax.numpy as jnp
from jax import lax
from jax.experimental import pallas as pl
from jax.experimental.pallas import tpu as pltpu
from jax.sharding import PartitionSpec as P

F32, BF16, I32 = jnp.float32, jnp.bfloat16, jnp.int32
MESH = pl.DeviceIdType.MESH
NX_DEV, NY_DEV, NZ_DEV = 4, 4, 8
BZ, BX = 16, 128
USED, SUP, NP = 48, 12, 4
ROWS = USED * SUP
PAD_ROWS = 640
OFFSETS = [(j // 9 - 1, (j // 3) % 3 - 1, j % 3 - 1) for j in range(27)]
FARTHEST = sorted(range(27), key=lambda j: -sum(abs(step) for step in OFFSETS[j]))
FACES = (4, 22, 10, 16, 12, 14)
PLANES = (0, 1, 14, 15)
PARTS = ((0, 48), (48, 40), (88, 40))
XO = 8
PX = BX + 16
CH = 16
C1 = -16.0 / 168.0
C2 = 1.0 / 168.0
C0 = -0.25 / 7.0


def split(value):
    high = value.astype(BF16)
    return high, (value - high.astype(F32)).astype(BF16)


def mm(a, b):
    return jnp.dot(a, b, preferred_element_type=F32)


def body(
    orb_hbm, pot_hbm, cnt_hbm, satom_hbm, sblock_hbm, proj_hbm, nle_hbm, outb,
    t0, t1, t2, halo, edge, pot, proj, pj, picks, cb, chi, clo, hot,
    qm, gt, gm, a48, g48, vals, p1, r1, v2, r2, ys, yr, xs, xr, erow,
    cnt, satom, sblock, nle, rowi,
    sem_y, sem_z, sem_in, zs, zr, xss, xrs, yss, yrs, s1s, s1r, s2s, s2r,
):
    gx, gy, gz = lax.axis_index("gx"), lax.axis_index("gy"), lax.axis_index("gz")

    def at(off):
        return (
            lax.rem(gx + (off[0] + NX_DEV), NX_DEV),
            lax.rem(gy + (off[1] + NY_DEV), NY_DEV),
            lax.rem(gz + (off[2] + NZ_DEV), NZ_DEV),
        )

    loads = [
        pltpu.make_async_copy(orb_hbm, t0.at[:, pl.ds(2, BZ), pl.ds(XO, BX), :], sem_in.at[0]),
        pltpu.make_async_copy(proj_hbm.at[0], proj, sem_in.at[1]),
        pltpu.make_async_copy(pot_hbm, pot, sem_in.at[2]),
        pltpu.make_async_copy(cnt_hbm, cnt, sem_in.at[3]),
        pltpu.make_async_copy(satom_hbm, satom, sem_in.at[4]),
        pltpu.make_async_copy(sblock_hbm, sblock, sem_in.at[5]),
        pltpu.make_async_copy(nle_hbm, nle, sem_in.at[6]),
    ]
    for copy in loads:
        copy.start()
    barrier = pltpu.get_barrier_semaphore()
    for j in FACES:
        pl.semaphore_signal(barrier, inc=1, device_id=at(OFFSETS[j]), device_id_type=MESH)

    def greet(sem, pair):
        for j in pair:
            pl.semaphore_signal(sem, inc=1, device_id=at(OFFSETS[j]), device_id_type=MESH)

    lane = lax.broadcasted_iota(I32, (8, 128), 1)
    lane_c = lax.broadcasted_iota(I32, (CH, 128), 1)
    sides = ((0, 0, 1), (0, 0, -1))

    def z_copy(k, t, up, part):
        first, count = PARTS[part]
        side = 0 if up else 1
        return pltpu.make_async_remote_copy(
            src_ref=t.at[:, pl.ds(BZ if up else 2, 2), pl.ds(XO + first, count), :],
            dst_ref=halo.at[k, side, :, :, pl.ds(first, count), :],
            send_sem=zs.at[k, side, part], recv_sem=zr.at[k, side, part],
            device_id=at((0, 0, 1 if up else -1)), device_id_type=MESH)

    def z_send(k, t, part):
        @pl.when(gz < NZ_DEV - 1)
        def _():
            z_copy(k, t, True, part).start()

        @pl.when(gz > 0)
        def _():
            z_copy(k, t, False, part).start()

    def z_receive(k, t, dest, factor):
        def add(o, z, value):
            here = pl.ds(XO, BX)
            dest[o, z + 2, here, :] = dest[o, z + 2, here, :] + value

        @pl.when(gz > 0)
        def _():
            for part in range(len(PARTS)):
                z_copy(k, t, True, part).wait_recv()
            for o in range(2):
                second, first = halo[k, 0, o, 0], halo[k, 0, o, 1]
                add(o, 0, (C1 * factor) * first + (C2 * factor) * second)
                add(o, 1, (C2 * factor) * first)

        @pl.when(gz < NZ_DEV - 1)
        def _():
            for part in range(len(PARTS)):
                z_copy(k, t, False, part).wait_recv()
            for o in range(2):
                first, second = halo[k, 1, o, 0], halo[k, 1, o, 1]
                add(o, BZ - 1, (C1 * factor) * first + (C2 * factor) * second)
                add(o, BZ - 2, (C2 * factor) * first)

    def z_sent(k, t):
        @pl.when(gz < NZ_DEV - 1)
        def _():
            for part in range(len(PARTS)):
                z_copy(k, t, True, part).wait_send()

        @pl.when(gz > 0)
        def _():
            for part in range(len(PARTS)):
                z_copy(k, t, False, part).wait_send()

    def xy_copies(k):
        made = []
        for d, step in ((0, 1), (1, -1)):
            made.append(pltpu.make_async_remote_copy(
                src_ref=xs.at[k, d], dst_ref=xr.at[k, d], send_sem=xss.at[k, d], recv_sem=xrs.at[k, d],
                device_id=at((step, 0, 0)), device_id_type=MESH))
            made.append(pltpu.make_async_remote_copy(
                src_ref=ys.at[k], dst_ref=yr.at[k, d], send_sem=yss.at[k, d], recv_sem=yrs.at[k, d],
                device_id=at((0, step, 0)), device_id_type=MESH))
        return made

    def xy_pack(k, t):
        def pack_y(pair, _):
            for half in range(2):
                z = 2 * pair + half
                parts = []
                for first in range(0, 32, 8):
                    packed = None
                    for q in range(first, first + 8):
                        rolled = pltpu.roll(
                            t[q // 16, z + 2, pl.ds(XO + 8 * (q % 16), 8), :], (4 * q + 2) % 128, 1)
                        packed = rolled if packed is None else jnp.where((lane >> 2) == q, rolled, packed)
                    parts.append(packed)
                low = jnp.where((lane >> 5) == 0, parts[0], parts[1])
                high = jnp.where((lane >> 5) == 2, parts[2], parts[3])
                ys[k, z] = jnp.where((lane >> 6) == 0, low, high)
            return 0

        def pack_x(pair, _):
            for half in range(2):
                for o in range(2):
                    q = half * 2 + o
                    xs[k, 0, pair, pl.ds(2 * q, 2), :] = t[o, 2 * pair + half + 2, pl.ds(XO + BX - 2, 2), :]
                    xs[k, 1, pair, pl.ds(2 * q, 2), :] = t[o, 2 * pair + half + 2, pl.ds(XO, 2), :]
            return 0

        lax.fori_loop(0, BZ // 2, pack_x, 0)
        lax.fori_loop(0, BZ // 2, pack_y, 0, unroll=2)
        for copy in xy_copies(k):
            copy.start()

    def xy_unpack(k, t):
        for copy in xy_copies(k):
            copy.wait_recv()

        def unpack_y(pair, _):
            for half in range(2):
                z = 2 * pair + half
                merged = jnp.where((lane & 3) < 2, yr[k, 0, z], yr[k, 1, z])
                for q in range(32):
                    edge[q // 16, z, pl.ds(8 * (q % 16), 8), :] = pltpu.roll(merged, (126 - 4 * q) % 128, 1)
            return 0

        def unpack_x(pair, _):
            for half in range(2):
                for o in range(2):
                    q = half * 2 + o
                    t[o, 2 * pair + half + 2, pl.ds(XO - 2, 2), :] = xr[k, 0, pair, pl.ds(2 * q, 2), :]
                    t[o, 2 * pair + half + 2, pl.ds(XO + BX, 2), :] = xr[k, 1, pair, pl.ds(2 * q, 2), :]
            return 0

        lax.fori_loop(0, BZ // 2, unpack_x, 0)
        lax.fori_loop(0, BZ // 2, unpack_y, 0, unroll=2)

    def first_round(k):
        made = []
        for j in FARTHEST:
            if j != 13:
                made.append(pltpu.make_async_remote_copy(
                    src_ref=p1.at[k, j], dst_ref=r1.at[k, 26 - j], send_sem=s1s.at[k], recv_sem=s1r.at[k],
                    device_id=at(OFFSETS[j]), device_id_type=MESH))
        return made

    def second_round(k):
        made = []
        for j in FARTHEST:
            if j != 13:
                made.append(pltpu.make_async_remote_copy(
                    src_ref=v2.at[k], dst_ref=r2.at[k, 26 - j], send_sem=s2s.at[k], recv_sem=s2r.at[k],
                    device_id=at(OFFSETS[j]), device_id_type=MESH))
        return made

    def all_rows(k, send, receive):
        return pltpu.make_async_remote_copy(
            src_ref=p1.at[k, pl.ds(0, 26)], dst_ref=r1.at[k, pl.ds(0, 26)], send_sem=send.at[k],
            recv_sem=receive.at[k], device_id=at((0, 0, 1)), device_id_type=MESH)

    def setup():
        def slot(k, state):
            j, s, jz = state
            above = gz + jz - 1
            live = (above >= 0) & (above < NZ_DEV)
            a48[pl.ds(k, 1), :] = jnp.full((1, 128), jnp.where(live, satom[0, s, j], -1000), I32)
            g48[pl.ds(k, 1), :] = jnp.full((1, 128), jnp.where(live, j, -1), I32)
            for i in range(SUP):
                block = sblock[0, i, s, j]
                rowi[i * USED + k] = block + (block >> 7) * (PX - BX) + (2 * PX + XO)
                pj[i, pl.ds(k, NP, stride=USED), :] = proj[j, s, :, pl.ds(i * 128, 128)]
            over = s + 1 >= cnt[0, j]
            later = jnp.where(jz == 2, 0, jz + 1)
            return (jnp.where(over, jnp.minimum(j + 1, 26), j), jnp.where(over, 0, s + 1),
                    jnp.where(over, later, jz))

        lax.fori_loop(0, USED, slot, (jnp.int32(0), jnp.int32(0), jnp.int32(0)))
        lane48 = lax.broadcasted_iota(I32, (USED, 128), 1)
        group_hot = jnp.where(g48[...] == lane48, 1.0, 0.0)
        for po in range(8):
            qm[pl.ds(po * USED, USED), :] = jnp.where(a48[...] * 8 + po == lane48, 1.0, 0.0)
            gt[pl.ds(po * USED, USED), :] = group_hot.astype(BF16)
        for c in range(3):
            tall = gt[pl.ds(c * 128, 128), :].astype(F32)
            gm[:, pl.ds(c * 128, 128)] = tall.T[:32].astype(BF16)
        row = jnp.zeros((1, 128), F32)
        lane1 = lax.broadcasted_iota(I32, (1, 128), 1)
        for a in range(16):
            for p in range(NP):
                row = jnp.where((lane1 >> 1) == a * NP + p, nle[p, a], row)
        erow[...] = row
        vals[...] = jnp.zeros_like(vals)
        chi[pl.ds(ROWS, PAD_ROWS - ROWS), :] = jnp.zeros((PAD_ROWS - ROWS, 256), BF16)
        clo[pl.ds(ROWS, PAD_ROWS - ROWS), :] = jnp.zeros((PAD_ROWS - ROWS, 256), BF16)
        plane = jnp.zeros((BX, 128), F32)

        for t in (t0, t1, t2):
            for o in range(2):
                for i in (0, 1, BZ + 2, BZ + 3):
                    t[o, i, pl.ds(XO, BX), :] = plane

    def setup_hot():
        lane1 = lax.broadcasted_iota(I32, (1, 128), 1)

        def fill(r, vectors):
            out = []
            for c in range(4):
                out.append(jnp.where(lane1 == r, rowi[c * 128 + r], vectors[c]))
            out.append(jnp.where((lane1 == r) & (r < ROWS - 512), rowi[jnp.minimum(512 + r, ROWS - 1)], vectors[4]))
            return tuple(out)

        vectors = lax.fori_loop(0, 128, fill, tuple(jnp.full((1, 128), -1, I32) for _ in range(5)), unroll=8)
        rows = lax.broadcasted_iota(I32, (BX, 128), 0)

        def plane(i, _):
            z = jnp.where(i < 2, i, jnp.where(i < 4, i + (BZ - 4), i - 2))
            for c in range(5):
                hot[i, :, pl.ds(c * 128, 128)] = jnp.where(
                    rows == vectors[c] - (z * PX + (2 * PX + XO)), 1.0, 0.0).astype(BF16)
            return 0

        lax.fori_loop(0, BZ, plane, 0)

    def coefficients(k, t):
        def gather(g, _):
            for s in range(8):
                row = rowi[g * 8 + s]
                for o in range(2):
                    picks[o, pl.ds(g * 8 + s, 1), :] = flat[o, pl.ds(row, 1), :]
            return 0

        flat = t.reshape(2, (BZ + 4) * PX, 128)
        lax.fori_loop(0, ROWS // 8, gather, 0, unroll=6)
        if k == 0:
            pl.semaphore_wait(sem_y, 2)
            greet(sem_z, (12, 14))

        def reduce(g, _):
            for o in range(2):
                sums = [None] * NP
                for i in range(SUP):
                    pick = picks[o, pl.ds(i * USED + g * 8, 8), :]
                    for p in range(NP):
                        term = pj[i, pl.ds(p * USED + g * 8, 8), :] * pick
                        sums[p] = term if sums[p] is None else sums[p] + term
                for p in range(NP):
                    cb[pl.ds((p * 2 + o) * USED + g * 8, 8), :] = sums[p]
            return 0

        lax.fori_loop(0, USED // 8, reduce, 0)
        ones = jnp.ones((128, 128), BF16)
        high, low = split(cb[...])
        spread = (mm(high, ones) + mm(low, ones)) * qm[...]
        high, low = split(spread)
        part = mm(gm[...], high) + mm(gm[...], low)
        for j in range(27):
            if j == 13:
                r1[k, 13] = part[13:14]
            else:
                p1[k, j] = part[j:j + 1]
        if k == 0:
            pl.semaphore_wait(sem_z, 2)
        for copy in first_round(k):
            copy.start()

    def totals(k):
        all_rows(k, s1s, s1r).wait_recv()
        row = r1[k, 0]
        for j in range(1, 27):
            row = row + r1[k, j]
        row = row * erow[...]
        v2[k] = row
        vals[pl.ds(13, 1), :] = row
        for copy in second_round(k):
            copy.start()

    def spread_values(k, factor):
        all_rows(k, s2s, s2r).wait_recv()
        for j in range(27):
            if j != 13:
                vals[pl.ds(j, 1), :] = r2[k, j]
        ones = jnp.ones((128, 128), BF16)
        high, low = split(vals[...] * factor)
        wide = (mm(gt[...], high) + mm(gt[...], low)) * qm[...]
        high, low = split(wide)
        cb[...] = mm(high, ones) + mm(low, ones)

        def expand(g, _):
            for o in range(2):
                weights = [cb[pl.ds((p * 2 + o) * USED + g * 16, 16), :] for p in range(NP)]
                for i in range(SUP):
                    total = weights[0] * pj[i, pl.ds(g * 16, 16), :]
                    for p in range(1, NP):
                        total = total + weights[p] * pj[i, pl.ds(p * USED + g * 16, 16), :]
                    high, low = split(total)
                    chi[pl.ds(i * USED + g * 16, 16), pl.ds(o * 128, 128)] = high
                    clo[pl.ds(i * USED + g * 16, 16), pl.ds(o * 128, 128)] = low
            return 0

        lax.fori_loop(0, USED // 16, expand, 0)

    def local_part(k, t, dest, before, z):
        def chunk(c, _):
            x0 = pl.multiple_of(c * CH, CH)
            here = pl.ds(XO + x0, CH)
            weight = pot[z, pl.ds(x0, CH), :] * (1.0 / 7.0) + C0
            for o in range(2):
                center = t[o, z + 2, here, :]
                e = edge[o, z, pl.ds(x0, CH), :]
                left = jnp.where(lane_c >= 126, e, center)
                right = jnp.where(lane_c < 2, e, center)
                near = (t[o, z + 1, here, :] + t[o, z + 3, here, :]) + (
                    t[o, z + 2, pl.ds(XO - 1 + x0, CH), :] + t[o, z + 2, pl.ds(XO + 1 + x0, CH), :])
                near = near + (pltpu.roll(jnp.where(lane_c == 127, e, center), 1, 1)
                               + pltpu.roll(jnp.where(lane_c == 0, e, center), 127, 1))
                far = (t[o, z, here, :] + t[o, z + 4, here, :]) + (
                    t[o, z + 2, pl.ds(XO - 2 + x0, CH), :] + t[o, z + 2, pl.ds(XO + 2 + x0, CH), :])
                far = far + (pltpu.roll(left, 2, 1) + pltpu.roll(right, 126, 1))
                value = C1 * near + C2 * far + weight * center
                if k == 0:
                    dest[o, z + 2, here, :] = value
                elif k == 1:
                    dest[o, z + 2, here, :] = 2.0 * value - before[o, z + 2, here, :]
                else:
                    dest[o, z + 2, here, :] = (
                        0.55 * t0[o, z + 2, here, :] - 0.44 * before[o, z + 2, here, :]
                        + 0.34 * center - 0.36 * value)
            return 0

        lax.fori_loop(0, BX // CH, chunk, 0, unroll=True)

    def add_nonlocal(k, dest, i, zs_of):
        four = hot[pl.ds(4 * i, 4)].reshape(4 * BX, PAD_ROWS)
        added = mm(four, chi[...]) + mm(four, clo[...])
        here = pl.ds(XO, BX)
        for n, z in enumerate(zs_of):
            rows = slice(n * BX, (n + 1) * BX)
            if k < 2:
                for o in range(2):
                    dest[o, z + 2, here, :] = dest[o, z + 2, here, :] + added[rows, o * 128:(o + 1) * 128]
            else:
                phi_a = dest[0, z + 2, here, :] + added[rows, :128]
                phi_b = dest[1, z + 2, here, :] + added[rows, 128:]
                outb[z] = 0.5 * (phi_a * phi_a + phi_b * phi_b)

    for copy in loads[3:]:
        copy.wait()
    loads[1].wait()
    setup()
    loads[0].wait()
    pl.semaphore_wait(barrier, len(FACES))
    z_send(0, t0, 0)
    greet(sem_y, (10, 16))
    factors = (1.0 / 7.0, 2.0 / 7.0, -0.36 / 7.0)
    states = ((t0, t1, None), (t1, t2, t0), (t2, t0, t1))
    for k in range(3):
        t, dest, before = states[k]
        coefficients(k, t)
        xy_pack(k, t)
        z_send(k, t, 1)
        if k == 0:
            loads[2].wait()
            setup_hot()
        totals(k)
        z_send(k, t, 2)
        xy_unpack(k, t)

        def inner(z, _):
            local_part(k, t, dest, before, z)
            return 0

        lax.fori_loop(0, BZ, inner, 0)
        spread_values(k, factors[k])
        z_receive(k, t, dest, (1.0, 2.0, -0.36)[k])
        add_nonlocal(k, dest, 0, PLANES)
        if k < 2:
            z_send(k + 1, dest, 0)

        def finish(i, _):
            add_nonlocal(k, dest, i, [4 * i - 2 + n for n in range(4)])
            return 0

        lax.fori_loop(1, 4, finish, 0)
        z_sent(k, t)
        for copy in xy_copies(k):
            copy.wait_send()
        all_rows(k, s1s, s1r).wait_send()
        all_rows(k, s2s, s2r).wait_send()


def per_device(orbitals, potential, counts, slot_atom, slot_block, projectors, nl_energy):
    vmem, smem, outside = pltpu.VMEM, pltpu.SMEM, pl.BlockSpec(memory_space=pltpu.HBM)
    field = vmem((2, BZ + 4, PX, 128), F32)
    dma = pltpu.SemaphoreType.DMA
    return pl.pallas_call(
        body,
        out_shape=jax.ShapeDtypeStruct(potential.shape, F32),
        in_specs=[outside] * 7,
        out_specs=pl.BlockSpec(memory_space=pltpu.VMEM),
        scratch_shapes=[
            field, field, field,
            vmem((3, 2, 2, 2, BX, 128), F32),
            vmem((2, BZ, BX, 128), F32),
            vmem((BZ, BX, 128), F32),
            vmem((27, 4, NP, SUP * 128), F32),
            vmem((SUP, NP * USED, 128), F32),
            vmem((2, ROWS, 128), F32),
            vmem((8 * USED, 128), F32),
            vmem((PAD_ROWS, 256), BF16), vmem((PAD_ROWS, 256), BF16),
            vmem((BZ, BX, PAD_ROWS), BF16),
            vmem((8 * USED, 128), F32), vmem((8 * USED, 128), BF16), vmem((32, 8 * USED), BF16),
            vmem((USED, 128), I32), vmem((USED, 128), I32),
            vmem((128, 128), F32),
            vmem((3, 27, 1, 128), F32), vmem((3, 27, 1, 128), F32),
            vmem((3, 1, 128), F32), vmem((3, 27, 1, 128), F32),
            vmem((3, BZ, 8, 128), F32), vmem((3, 2, BZ, 8, 128), F32),
            vmem((3, 2, BZ // 2, 8, 128), F32), vmem((3, 2, BZ // 2, 8, 128), F32),
            vmem((1, 128), F32),
            smem((1, 27), I32), smem((1, 4, 27), I32), smem((1, SUP, 4, 27), I32), smem((NP, 16), F32),
            smem((ROWS,), I32),
            pltpu.SemaphoreType.REGULAR, pltpu.SemaphoreType.REGULAR, dma((7,)),
            dma((3, 2, 3)), dma((3, 2, 3)), dma((3, 2)), dma((3, 2)), dma((3, 2)), dma((3, 2)),
            dma((3,)), dma((3,)), dma((3,)), dma((3,)),
        ],
        compiler_params=pltpu.CompilerParams(
            collective_id=0, has_side_effects=True, vmem_limit_bytes=63 * 1024 * 1024
        ),
    )(orbitals, potential, counts, slot_atom.transpose(0, 2, 1), slot_block.transpose(0, 3, 2, 1), projectors,
      nl_energy.T)


def solution(mesh):
    in_specs = (
        P(None, "gz", "gx", "gy"),
        P("gz", "gx", "gy"),
        P(("gx", "gy", "gz"), None),
        P(("gx", "gy", "gz"), None, None),
        P(("gx", "gy", "gz"), None, None, None),
        P(("gx", "gy", "gz"), None, None, None, None),
        P(("gx", "gy", "gz"), None),
    )
    out_specs = P("gz", "gx", "gy")
    return jax.shard_map(
        per_device, mesh=mesh, in_specs=in_specs, out_specs=out_specs, check_vma=False
    )
```

```python
import jax
import jax.numpy as jnp
from jax import lax
from jax.experimental import pallas as pl
from jax.experimental.pallas import tpu as pltpu
from jax.sharding import PartitionSpec as P

F32, BF16, I32 = jnp.float32, jnp.bfloat16, jnp.int32
MESH = pl.DeviceIdType.MESH
NX_DEV, NY_DEV, NZ_DEV = 4, 4, 8
BZ, BX = 16, 128
USED, SUP, NP = 48, 12, 4
ROWS = USED * SUP
PAD_ROWS = 640
OFFSETS = [(j // 9 - 1, (j // 3) % 3 - 1, j % 3 - 1) for j in range(27)]
FARTHEST = sorted(range(27), key=lambda j: -sum(abs(step) for step in OFFSETS[j]))
FACES = (4, 22, 10, 16, 12, 14)
PLANES = (0, 1, 14, 15)
PARTS = ((0, 48), (48, 40), (88, 40))
XO = 8
PX = BX + 16
CH = 16
C1 = -16.0 / 168.0
C2 = 1.0 / 168.0
C0 = -0.25 / 7.0


def split(value):
    high = value.astype(BF16)
    return high, (value - high.astype(F32)).astype(BF16)


def mm(a, b):
    return jnp.dot(a, b, preferred_element_type=F32)


def body(
    orb_hbm, pot_hbm, cnt_hbm, satom_hbm, sblock_hbm, proj_hbm, nle_hbm, outb,
    t0, t1, t2, halo, edge, pot, proj, pj, picks, cb, chi, clo, hot,
    qm, gt, gm, a48, g48, vals, p1, r1, v2, r2, ys, yr, xs, xr, erow,
    cnt, satom, sblock, nle, rowi,
    sem_y, sem_z, sem_in, zs, zr, xss, xrs, yss, yrs, s1s, s1r, s2s, s2r,
):
    gx, gy, gz = lax.axis_index("gx"), lax.axis_index("gy"), lax.axis_index("gz")

    def at(off):
        return (
            lax.rem(gx + (off[0] + NX_DEV), NX_DEV),
            lax.rem(gy + (off[1] + NY_DEV), NY_DEV),
            lax.rem(gz + (off[2] + NZ_DEV), NZ_DEV),
        )

    loads = [
        pltpu.make_async_copy(orb_hbm, t0.at[:, pl.ds(2, BZ), pl.ds(XO, BX), :], sem_in.at[0]),
        pltpu.make_async_copy(proj_hbm.at[0], proj, sem_in.at[1]),
        pltpu.make_async_copy(pot_hbm, pot, sem_in.at[2]),
        pltpu.make_async_copy(cnt_hbm, cnt, sem_in.at[3]),
        pltpu.make_async_copy(satom_hbm, satom, sem_in.at[4]),
        pltpu.make_async_copy(sblock_hbm, sblock, sem_in.at[5]),
        pltpu.make_async_copy(nle_hbm, nle, sem_in.at[6]),
    ]
    for copy in loads:
        copy.start()
    barrier = pltpu.get_barrier_semaphore()
    for j in FACES:
        pl.semaphore_signal(barrier, inc=1, device_id=at(OFFSETS[j]), device_id_type=MESH)

    def greet(sem, pair):
        for j in pair:
            pl.semaphore_signal(sem, inc=1, device_id=at(OFFSETS[j]), device_id_type=MESH)

    lane = lax.broadcasted_iota(I32, (8, 128), 1)
    lane_c = lax.broadcasted_iota(I32, (CH, 128), 1)
    sides = ((0, 0, 1), (0, 0, -1))

    def z_copy(k, t, up, part):
        first, count = PARTS[part]
        side = 0 if up else 1
        return pltpu.make_async_remote_copy(
            src_ref=t.at[:, pl.ds(BZ if up else 2, 2), pl.ds(XO + first, count), :],
            dst_ref=halo.at[k, side, :, :, pl.ds(first, count), :],
            send_sem=zs.at[k, side, part], recv_sem=zr.at[k, side, part],
            device_id=at((0, 0, 1 if up else -1)), device_id_type=MESH)

    def z_send(k, t, part):
        @pl.when(gz < NZ_DEV - 1)
        def _():
            z_copy(k, t, True, part).start()

        @pl.when(gz > 0)
        def _():
            z_copy(k, t, False, part).start()

    def z_receive(k, t, dest, factor):
        def add(o, z, value):
            here = pl.ds(XO, BX)
            dest[o, z + 2, here, :] = dest[o, z + 2, here, :] + value

        @pl.when(gz > 0)
        def _():
            for part in range(len(PARTS)):
                z_copy(k, t, True, part).wait_recv()
            for o in range(2):
                second, first = halo[k, 0, o, 0], halo[k, 0, o, 1]
                add(o, 0, (C1 * factor) * first + (C2 * factor) * second)
                add(o, 1, (C2 * factor) * first)

        @pl.when(gz < NZ_DEV - 1)
        def _():
            for part in range(len(PARTS)):
                z_copy(k, t, False, part).wait_recv()
            for o in range(2):
                first, second = halo[k, 1, o, 0], halo[k, 1, o, 1]
                add(o, BZ - 1, (C1 * factor) * first + (C2 * factor) * second)
                add(o, BZ - 2, (C2 * factor) * first)

    def z_sent(k, t):
        @pl.when(gz < NZ_DEV - 1)
        def _():
            for part in range(len(PARTS)):
                z_copy(k, t, True, part).wait_send()

        @pl.when(gz > 0)
        def _():
            for part in range(len(PARTS)):
                z_copy(k, t, False, part).wait_send()

    def xy_copies(k):
        made = []
        for d, step in ((0, 1), (1, -1)):
            made.append(pltpu.make_async_remote_copy(
                src_ref=xs.at[k, d], dst_ref=xr.at[k, d], send_sem=xss.at[k, d], recv_sem=xrs.at[k, d],
                device_id=at((step, 0, 0)), device_id_type=MESH))
            made.append(pltpu.make_async_remote_copy(
                src_ref=ys.at[k], dst_ref=yr.at[k, d], send_sem=yss.at[k, d], recv_sem=yrs.at[k, d],
                device_id=at((0, step, 0)), device_id_type=MESH))
        return made

    def xy_pack(k, t):
        def pack_y(pair, _):
            for half in range(2):
                z = 2 * pair + half
                parts = []
                for first in range(0, 32, 8):
                    packed = None
                    for q in range(first, first + 8):
                        rolled = pltpu.roll(
                            t[q // 16, z + 2, pl.ds(XO + 8 * (q % 16), 8), :], (4 * q + 2) % 128, 1)
                        packed = rolled if packed is None else jnp.where((lane >> 2) == q, rolled, packed)
                    parts.append(packed)
                low = jnp.where((lane >> 5) == 0, parts[0], parts[1])
                high = jnp.where((lane >> 5) == 2, parts[2], parts[3])
                ys[k, z] = jnp.where((lane >> 6) == 0, low, high)
            return 0

        def pack_x(pair, _):
            for half in range(2):
                for o in range(2):
                    q = half * 2 + o
                    xs[k, 0, pair, pl.ds(2 * q, 2), :] = t[o, 2 * pair + half + 2, pl.ds(XO + BX - 2, 2), :]
                    xs[k, 1, pair, pl.ds(2 * q, 2), :] = t[o, 2 * pair + half + 2, pl.ds(XO, 2), :]
            return 0

        lax.fori_loop(0, BZ // 2, pack_x, 0)
        lax.fori_loop(0, BZ // 2, pack_y, 0, unroll=2)
        for copy in xy_copies(k):
            copy.start()

    def xy_unpack(k, t):
        for copy in xy_copies(k):
            copy.wait_recv()

        def unpack_y(pair, _):
            for half in range(2):
                z = 2 * pair + half
                merged = jnp.where((lane & 3) < 2, yr[k, 0, z], yr[k, 1, z])
                for q in range(32):
                    edge[q // 16, z, pl.ds(8 * (q % 16), 8), :] = pltpu.roll(merged, (126 - 4 * q) % 128, 1)
            return 0

        def unpack_x(pair, _):
            for half in range(2):
                for o in range(2):
                    q = half * 2 + o
                    t[o, 2 * pair + half + 2, pl.ds(XO - 2, 2), :] = xr[k, 0, pair, pl.ds(2 * q, 2), :]
                    t[o, 2 * pair + half + 2, pl.ds(XO + BX, 2), :] = xr[k, 1, pair, pl.ds(2 * q, 2), :]
            return 0

        lax.fori_loop(0, BZ // 2, unpack_x, 0)
        lax.fori_loop(0, BZ // 2, unpack_y, 0, unroll=2)

    def first_round(k):
        made = []
        for j in FARTHEST:
            if j != 13:
                made.append(pltpu.make_async_remote_copy(
                    src_ref=p1.at[k, j], dst_ref=r1.at[k, 26 - j], send_sem=s1s.at[k], recv_sem=s1r.at[k],
                    device_id=at(OFFSETS[j]), device_id_type=MESH))
        return made

    def second_round(k):
        made = []
        for j in FARTHEST:
            if j != 13:
                made.append(pltpu.make_async_remote_copy(
                    src_ref=v2.at[k], dst_ref=r2.at[k, 26 - j], send_sem=s2s.at[k], recv_sem=s2r.at[k],
                    device_id=at(OFFSETS[j]), device_id_type=MESH))
        return made

    def all_rows(k, send, receive):
        return pltpu.make_async_remote_copy(
            src_ref=p1.at[k, pl.ds(0, 26)], dst_ref=r1.at[k, pl.ds(0, 26)], send_sem=send.at[k],
            recv_sem=receive.at[k], device_id=at((0, 0, 1)), device_id_type=MESH)

    def setup():
        def slot(k, state):
            j, s, jz = state
            above = gz + jz - 1
            live = (above >= 0) & (above < NZ_DEV)
            a48[pl.ds(k, 1), :] = jnp.full((1, 128), jnp.where(live, satom[0, s, j], -1000), I32)
            g48[pl.ds(k, 1), :] = jnp.full((1, 128), jnp.where(live, j, -1), I32)
            for i in range(SUP):
                block = sblock[0, i, s, j]
                rowi[i * USED + k] = block + (block >> 7) * (PX - BX) + (2 * PX + XO)
                pj[i, pl.ds(k, NP, stride=USED), :] = proj[j, s, :, pl.ds(i * 128, 128)]
            over = s + 1 >= cnt[0, j]
            later = jnp.where(jz == 2, 0, jz + 1)
            return (jnp.where(over, jnp.minimum(j + 1, 26), j), jnp.where(over, 0, s + 1),
                    jnp.where(over, later, jz))

        lax.fori_loop(0, USED, slot, (jnp.int32(0), jnp.int32(0), jnp.int32(0)))
        lane48 = lax.broadcasted_iota(I32, (USED, 128), 1)
        group_hot = jnp.where(g48[...] == lane48, 1.0, 0.0)
        for po in range(8):
            qm[pl.ds(po * USED, USED), :] = jnp.where(a48[...] * 8 + po == lane48, 1.0, 0.0)
            gt[pl.ds(po * USED, USED), :] = group_hot.astype(BF16)
        for c in range(3):
            tall = gt[pl.ds(c * 128, 128), :].astype(F32)
            gm[:, pl.ds(c * 128, 128)] = tall.T[:32].astype(BF16)
        row = jnp.zeros((1, 128), F32)
        lane1 = lax.broadcasted_iota(I32, (1, 128), 1)
        for a in range(16):
            for p in range(NP):
                row = jnp.where((lane1 >> 1) == a * NP + p, nle[p, a], row)
        erow[...] = row
        vals[...] = jnp.zeros_like(vals)
        chi[pl.ds(ROWS, PAD_ROWS - ROWS), :] = jnp.zeros((PAD_ROWS - ROWS, 256), BF16)
        clo[pl.ds(ROWS, PAD_ROWS - ROWS), :] = jnp.zeros((PAD_ROWS - ROWS, 256), BF16)
        plane = jnp.zeros((BX, 128), F32)

        for t in (t0, t1, t2):
            for o in range(2):
                for i in (0, 1, BZ + 2, BZ + 3):
                    t[o, i, pl.ds(XO, BX), :] = plane

    def setup_hot():
        lane1 = lax.broadcasted_iota(I32, (1, 128), 1)

        def fill(r, vectors):
            out = []
            for c in range(4):
                out.append(jnp.where(lane1 == r, rowi[c * 128 + r], vectors[c]))
            out.append(jnp.where((lane1 == r) & (r < ROWS - 512), rowi[jnp.minimum(512 + r, ROWS - 1)], vectors[4]))
            return tuple(out)

        vectors = lax.fori_loop(0, 128, fill, tuple(jnp.full((1, 128), -1, I32) for _ in range(5)), unroll=8)
        rows = lax.broadcasted_iota(I32, (BX, 128), 0)

        def plane(i, _):
            z = jnp.where(i < 2, i, jnp.where(i < 4, i + (BZ - 4), i - 2))
            for c in range(5):
                hot[i, :, pl.ds(c * 128, 128)] = jnp.where(
                    rows == vectors[c] - (z * PX + (2 * PX + XO)), 1.0, 0.0).astype(BF16)
            return 0

        lax.fori_loop(0, BZ, plane, 0)

    def coefficients(k, t):
        def gather(g, _):
            for s in range(8):
                row = rowi[g * 8 + s]
                for o in range(2):
                    picks[o, pl.ds(g * 8 + s, 1), :] = flat[o, pl.ds(row, 1), :]
            return 0

        flat = t.reshape(2, (BZ + 4) * PX, 128)
        lax.fori_loop(0, ROWS // 8, gather, 0, unroll=6)
        if k == 0:
            pl.semaphore_wait(sem_y, 2)
            greet(sem_z, (12, 14))

        def reduce(g, _):
            for o in range(2):
                sums = [None] * NP
                for i in range(SUP):
                    pick = picks[o, pl.ds(i * USED + g * 8, 8), :]
                    for p in range(NP):
                        term = pj[i, pl.ds(p * USED + g * 8, 8), :] * pick
                        sums[p] = term if sums[p] is None else sums[p] + term
                for p in range(NP):
                    cb[pl.ds((p * 2 + o) * USED + g * 8, 8), :] = sums[p]
            return 0

        lax.fori_loop(0, USED // 8, reduce, 0, unroll=3)
        ones = jnp.ones((128, 128), BF16)
        high, low = split(cb[...])
        spread = (mm(high, ones) + mm(low, ones)) * qm[...]
        high, low = split(spread)
        part = mm(gm[...], high) + mm(gm[...], low)
        for j in range(27):
            if j == 13:
                r1[k, 13] = part[13:14]
            else:
                p1[k, j] = part[j:j + 1]
        if k == 0:
            pl.semaphore_wait(sem_z, 2)
        for copy in first_round(k):
            copy.start()

    def totals(k):
        all_rows(k, s1s, s1r).wait_recv()
        row = r1[k, 0]
        for j in range(1, 27):
            row = row + r1[k, j]
        row = row * erow[...]
        v2[k] = row
        vals[pl.ds(13, 1), :] = row
        for copy in second_round(k):
            copy.start()

    def spread_values(k, factor):
        all_rows(k, s2s, s2r).wait_recv()
        for j in range(27):
            if j != 13:
                vals[pl.ds(j, 1), :] = r2[k, j]
        ones = jnp.ones((128, 128), BF16)
        high, low = split(vals[...] * factor)
        wide = (mm(gt[...], high) + mm(gt[...], low)) * qm[...]
        high, low = split(wide)
        cb[...] = mm(high, ones) + mm(low, ones)

        def expand(g, _):
            for o in range(2):
                weights = [cb[pl.ds((p * 2 + o) * USED + g * 16, 16), :] for p in range(NP)]
                for i in range(SUP):
                    total = weights[0] * pj[i, pl.ds(g * 16, 16), :]
                    for p in range(1, NP):
                        total = total + weights[p] * pj[i, pl.ds(p * USED + g * 16, 16), :]
                    high, low = split(total)
                    chi[pl.ds(i * USED + g * 16, 16), pl.ds(o * 128, 128)] = high
                    clo[pl.ds(i * USED + g * 16, 16), pl.ds(o * 128, 128)] = low
            return 0

        lax.fori_loop(0, USED // 16, expand, 0, unroll=True)

    def local_part(k, t, dest, before, z):
        def chunk(c, _):
            x0 = pl.multiple_of(c * CH, CH)
            here = pl.ds(XO + x0, CH)
            weight = pot[z, pl.ds(x0, CH), :] * (1.0 / 7.0) + C0
            for o in range(2):
                center = t[o, z + 2, here, :]
                e = edge[o, z, pl.ds(x0, CH), :]
                left = jnp.where(lane_c >= 126, e, center)
                right = jnp.where(lane_c < 2, e, center)
                near = (t[o, z + 1, here, :] + t[o, z + 3, here, :]) + (
                    t[o, z + 2, pl.ds(XO - 1 + x0, CH), :] + t[o, z + 2, pl.ds(XO + 1 + x0, CH), :])
                near = near + (pltpu.roll(jnp.where(lane_c == 127, e, center), 1, 1)
                               + pltpu.roll(jnp.where(lane_c == 0, e, center), 127, 1))
                far = (t[o, z, here, :] + t[o, z + 4, here, :]) + (
                    t[o, z + 2, pl.ds(XO - 2 + x0, CH), :] + t[o, z + 2, pl.ds(XO + 2 + x0, CH), :])
                far = far + (pltpu.roll(left, 2, 1) + pltpu.roll(right, 126, 1))
                value = C1 * near + C2 * far + weight * center
                if k == 0:
                    dest[o, z + 2, here, :] = value
                elif k == 1:
                    dest[o, z + 2, here, :] = 2.0 * value - before[o, z + 2, here, :]
                else:
                    dest[o, z + 2, here, :] = (
                        0.55 * t0[o, z + 2, here, :] - 0.44 * before[o, z + 2, here, :]
                        + 0.34 * center - 0.36 * value)
            return 0

        lax.fori_loop(0, BX // CH, chunk, 0, unroll=True)

    def add_nonlocal(k, dest, i, zs_of):
        four = hot[pl.ds(4 * i, 4)].reshape(4 * BX, PAD_ROWS)
        added = mm(four, chi[...]) + mm(four, clo[...])
        here = pl.ds(XO, BX)
        for n, z in enumerate(zs_of):
            rows = slice(n * BX, (n + 1) * BX)
            if k < 2:
                for o in range(2):
                    dest[o, z + 2, here, :] = dest[o, z + 2, here, :] + added[rows, o * 128:(o + 1) * 128]
            else:
                phi_a = dest[0, z + 2, here, :] + added[rows, :128]
                phi_b = dest[1, z + 2, here, :] + added[rows, 128:]
                outb[z] = 0.5 * (phi_a * phi_a + phi_b * phi_b)

    for copy in loads[3:]:
        copy.wait()
    loads[1].wait()
    setup()
    loads[0].wait()
    pl.semaphore_wait(barrier, len(FACES))
    z_send(0, t0, 0)
    greet(sem_y, (10, 16))
    factors = (1.0 / 7.0, 2.0 / 7.0, -0.36 / 7.0)
    states = ((t0, t1, None), (t1, t2, t0), (t2, t0, t1))
    for k in range(3):
        t, dest, before = states[k]
        coefficients(k, t)
        xy_pack(k, t)
        z_send(k, t, 1)
        if k == 0:
            loads[2].wait()
            setup_hot()
        totals(k)
        z_send(k, t, 2)
        xy_unpack(k, t)

        def inner(z, _):
            local_part(k, t, dest, before, z)
            return 0

        lax.fori_loop(0, BZ, inner, 0)
        spread_values(k, factors[k])
        z_receive(k, t, dest, (1.0, 2.0, -0.36)[k])
        add_nonlocal(k, dest, 0, PLANES)
        if k < 2:
            z_send(k + 1, dest, 0)

        def finish(i, _):
            add_nonlocal(k, dest, i, [4 * i - 2 + n for n in range(4)])
            return 0

        lax.fori_loop(1, 4, finish, 0)
        z_sent(k, t)
        for copy in xy_copies(k):
            copy.wait_send()
        all_rows(k, s1s, s1r).wait_send()
        all_rows(k, s2s, s2r).wait_send()


def per_device(orbitals, potential, counts, slot_atom, slot_block, projectors, nl_energy):
    vmem, smem, outside = pltpu.VMEM, pltpu.SMEM, pl.BlockSpec(memory_space=pltpu.HBM)
    field = vmem((2, BZ + 4, PX, 128), F32)
    dma = pltpu.SemaphoreType.DMA
    return pl.pallas_call(
        body,
        out_shape=jax.ShapeDtypeStruct(potential.shape, F32),
        in_specs=[outside] * 7,
        out_specs=pl.BlockSpec(memory_space=pltpu.VMEM),
        scratch_shapes=[
            field, field, field,
            vmem((3, 2, 2, 2, BX, 128), F32),
            vmem((2, BZ, BX, 128), F32),
            vmem((BZ, BX, 128), F32),
            vmem((27, 4, NP, SUP * 128), F32),
            vmem((SUP, NP * USED, 128), F32),
            vmem((2, ROWS, 128), F32),
            vmem((8 * USED, 128), F32),
            vmem((PAD_ROWS, 256), BF16), vmem((PAD_ROWS, 256), BF16),
            vmem((BZ, BX, PAD_ROWS), BF16),
            vmem((8 * USED, 128), F32), vmem((8 * USED, 128), BF16), vmem((32, 8 * USED), BF16),
            vmem((USED, 128), I32), vmem((USED, 128), I32),
            vmem((128, 128), F32),
            vmem((3, 27, 1, 128), F32), vmem((3, 27, 1, 128), F32),
            vmem((3, 1, 128), F32), vmem((3, 27, 1, 128), F32),
            vmem((3, BZ, 8, 128), F32), vmem((3, 2, BZ, 8, 128), F32),
            vmem((3, 2, BZ // 2, 8, 128), F32), vmem((3, 2, BZ // 2, 8, 128), F32),
            vmem((1, 128), F32),
            smem((1, 27), I32), smem((1, 4, 27), I32), smem((1, SUP, 4, 27), I32), smem((NP, 16), F32),
            smem((ROWS,), I32),
            pltpu.SemaphoreType.REGULAR, pltpu.SemaphoreType.REGULAR, dma((7,)),
            dma((3, 2, 3)), dma((3, 2, 3)), dma((3, 2)), dma((3, 2)), dma((3, 2)), dma((3, 2)),
            dma((3,)), dma((3,)), dma((3,)), dma((3,)),
        ],
        compiler_params=pltpu.CompilerParams(
            collective_id=0, has_side_effects=True, vmem_limit_bytes=63 * 1024 * 1024
        ),
    )(orbitals, potential, counts, slot_atom.transpose(0, 2, 1), slot_block.transpose(0, 3, 2, 1), projectors,
      nl_energy.T)


def solution(mesh):
    in_specs = (
        P(None, "gz", "gx", "gy"),
        P("gz", "gx", "gy"),
        P(("gx", "gy", "gz"), None),
        P(("gx", "gy", "gz"), None, None),
        P(("gx", "gy", "gz"), None, None, None),
        P(("gx", "gy", "gz"), None, None, None, None),
        P(("gx", "gy", "gz"), None),
    )
    out_specs = P("gz", "gx", "gy")
    return jax.shard_map(
        per_device, mesh=mesh, in_specs=in_specs, out_specs=out_specs, check_vma=False
    )
```
